256 devices in a mesh: ctx: 8 (over x, core), exp: 32 (over y, z).
Axes of the slice: x: 4, y: 4, z: 8, core: 2. Of those that a mesh axis runs over, the one named last changes fastest.
Arguments:
- logits: bfloat16 [1024, 81920], P('ctx', 'exp'), may hold values from -16 to 250
- head_weight: bfloat16 [81920, 7168], P('exp', 'ctx'), may hold values from -0.0625 to 0.0625
- token_ids: int32 [1024], P('ctx'), may hold values from 0 to 81919
- slab_order: int32 [16], replicated, may hold values from 0 to 15, each once
- token_weights: float32 [1024], P('ctx'), may hold values from 4 to 64
- moe_input: bfloat16 [1024, 7168], P('exp', 'ctx'), may hold values from -6 to 6
- routes: int32 [1024, 8], P('exp'), may hold values from 0 to 31, all different within a row; in each aligned block of 32 rows (0 to 31, 32 to 63, ...) at most 16 rows name the same one
- probs: bfloat16 [1024, 8], P('exp'), may hold values from 0.049804688 to 1
- w_gate: bfloat16 [32, 7168, 1024], P('exp', 'ctx'), may hold values from -0.0625 to 0.0625
- w_up: bfloat16 [32, 7168, 1024], P('exp', 'ctx'), may hold values from -0.0625 to 0.0625
- w_down: bfloat16 [32, 1024, 7168], P('exp', None, 'ctx'), may hold values from -0.1875 to 0.1875
Outputs:
- d_x: float32 [1024, 7168], P('exp', 'ctx')
- d_prob: float32 [1024, 8], P('exp')
The draws below stay inside these ranges and needn't reach their ends.
Inputs may be any that keep to these rules, and one draw needn't show every extreme that they name: `slab_order`: a permutation of the 16 slabs. `routes`: each row names 8 different experts; among the rows of one exp index (32 rows) no expert is named more than 16 times, a bound that some block reaches.
All inputs are finite; a program needn't handle non-finite values.
Results may differ from the reference program's by a relative error of at most 0.0042.
Values may be sent and summed in bfloat16 or wider, within the bound.
No kernel may reach another device: no remote copies, remote signals or barrier semaphores. Data moves between devices by JAX's collectives and lax.ppermute only.
A program may use at most 64 MiB of HBM per device.

```python
import math
import jax
import jax.numpy as jnp
import numpy as np
from jax import lax

D = 7168
FFN = 1024
TOP = 8
SLAB = 64
SLABS = 16
SEQ = 1024
VOCAB = 81920
EXPERTS = 32
TOK_EXP = 32
CAP = 16
N_EXP = 32


def draw_logits(key, part):
    key = jax.random.fold_in(key, 7)
    first_key = jax.random.fold_in(key, 0)
    columns = jnp.arange(VOCAB, dtype=jnp.int32)
    ramp = (jnp.log(3.0) * columns.astype(jnp.float32) / VOCAB)[None, :]
    return (jnp.clip(3.0 * jax.random.normal(first_key, (SEQ, VOCAB), jnp.float32), -15.0, 15.0) + ramp).astype(jnp.bfloat16)


def place_ends(result, rng, smallest, high):
    longest = result.shape.index(max(result.shape))
    spots = []
    for shift in (0, 1):
        where = [jax.random.randint(jax.random.fold_in(rng, axis), (), 0, length) for axis, length in enumerate(result.shape)]
        where[longest] = (where[longest] + shift) % result.shape[longest]
        spots.append(tuple(where))
    return result.at[spots[0]].set(smallest).at[spots[1]].set(high)


def levels(stream_key, extent, cuts, least, top_value):
    factor_of = 1.0
    for dim, blocks in cuts:
        steps = jax.random.uniform(jax.random.fold_in(jax.random.fold_in(stream_key, 6), dim), (blocks,), jnp.float32, least / len(cuts), top_value / len(cuts))
        factor_of = factor_of * jnp.repeat(jnp.exp(steps), extent[dim] // blocks).reshape((-1,) + (1,) * (len(extent) - 1 - dim))
    return factor_of


def ranked_wide(stream_key, dims, number_of, skew):
    loads = [min(1 << octave, number_of + 1 - (1 << octave)) * (1 << 20) // math.isqrt((1 << octave) ** skew) + 1 for octave in range((number_of + 1).bit_length()) if 1 << octave <= number_of]
    spread = 1 + sum(loads) // (1 << 30)
    grid = np.cumsum(np.array([max(1, weight // spread) for weight in loads]))
    pick = jax.random.randint(jax.random.fold_in(stream_key, 1), dims, 0, int(grid[len(loads) - 1]))
    start = jnp.left_shift(1, jnp.searchsorted(jnp.asarray(grid, jnp.int32), pick, side="right").astype(jnp.int32))
    grade = start - 1 + jax.random.randint(jax.random.fold_in(stream_key, 4), dims, 0, 1 << 30) % jnp.minimum(start, number_of + 1 - start)
    return jax.random.permutation(jax.random.fold_in(stream_key, 2), number_of)[grade].astype(jnp.int32)


def assign_block(stream_key, own, number, rows, count, top, reach, skew):
    sequence = jax.random.permutation(stream_key, count)
    crowded, common = load_shares(count, rows * top, reach, skew, True), load_shares(count, rows * top, reach, skew, False)
    places = jnp.arange(count)

    def named(tallies, rotation):
        used = int((tallies > 0).sum())
        fixed = max(1, used // 4)
        passed = fixed + (places - fixed + rotation * (used - fixed)) % max(1, count - fixed)
        return jnp.zeros((count,), jnp.int32).at[sequence[jnp.where(places < fixed, places, passed)]].set(jnp.asarray(tallies, jnp.int32))

    tallies = jnp.where(number % 4 == 0, named(crowded, number // 4), named(common, number - number // 4 - 1))
    mixed = jax.random.permutation(jax.random.fold_in(own, 3), count)
    source_of, taker = mixed[0:count // 2 * 2:2], mixed[1:count // 2 * 2:2]
    room = jnp.minimum(tallies[source_of] - 1, reach - tallies[taker]) // 2
    room = jnp.where((source_of == sequence[0]) | (taker == sequence[0]) | (tallies[taker] == 0), 0, jnp.maximum(room, 0))
    passed = jax.random.randint(jax.random.fold_in(own, 4), (count // 2,), 0, 1 << 20) % (room + 1)
    tallies = tallies.at[source_of].add(-passed).at[taker].add(passed)
    members = jnp.searchsorted(jnp.cumsum(tallies), jnp.arange(rows * top), side="right").astype(jnp.int32)
    table = members.reshape(top, rows).T
    table = table[jax.random.permutation(jax.random.fold_in(own, 1), rows)]
    rotation = jax.random.randint(jax.random.fold_in(own, 2), (rows, 1), 0, top)
    return jnp.take_along_axis(table, (jnp.arange(top)[None, :] + rotation) % top, axis=1)


def load_shares(number_of, total, most, lean, full):
    portions = [(1 << 20) // math.isqrt(standing ** lean) + 1 for standing in range(1, number_of + 1)]
    largest = most if full else min(most, max(-(-total // number_of), total * portions[0] // sum(portions)))
    least = 1 if total - largest >= number_of - 1 else 0
    counts, rest = [largest] + [least] * (number_of - 1), total - largest - least * (number_of - 1)
    while rest > 0:
        movable = [i for i in range(1, number_of) if counts[i] < largest] or [i for i in range(1, number_of) if counts[i] < most]
        whole, left = sum([portions[i] for i in movable]), rest
        for i in movable:
            addition = min(most - counts[i], max(1, left * portions[i] // whole), rest)
            counts[i] = counts[i] + addition
            rest = rest - addition
    return np.array(counts)


def centred(rng, extent, width, reach, pieces=(), kind=jnp.bfloat16):
    drawn = jax.random.normal(rng, extent, jnp.float32) * width
    if len(pieces) > 0:
        drawn = levels(rng, extent, pieces, -0.22, 0.18) * drawn
    return jnp.clip(drawn, min=-reach, max=reach).astype(kind)


def setup_inputs(seed: int = 0) -> dict:
    keys = jax.random.split(jax.random.key(seed), 12)
    logits = draw_logits(jax.random.fold_in(keys[11], 71), 0)
    head_weight = centred(keys[1], (VOCAB, D), D ** -0.5, 0.0625, ((0, 32), (1, 8)))
    token_ids = place_ends(ranked_wide(keys[2], (SEQ,), VOCAB, 2), jax.random.fold_in(keys[2], 3), 0, VOCAB - 1).astype(jnp.int32)
    slab_order = jax.random.permutation(keys[3], SLABS).astype(jnp.int32)
    token_weights = jnp.clip(jnp.exp(math.log(64.0) - 2.7725887 * jax.random.uniform(keys[4], (SEQ,), jnp.float32) ** levels(keys[4], (SEQ,), ((0, 8),), -0.2, 0.2)), 4.0, 64.0)
    moe_input = centred(keys[5], (SEQ, D), 1.0, 6.0, ((0, 32), (1, 8)))
    routes_keys = jax.random.split(jax.random.fold_in(keys[6], 1), SEQ // TOK_EXP)
    routes_turns = jax.random.permutation(jax.random.fold_in(keys[6], 3), SEQ // TOK_EXP)
    routes = jax.vmap(lambda own, number: assign_block(jax.random.fold_in(keys[6], 2), own, number, TOK_EXP, EXPERTS, TOP, CAP, 2))(routes_keys, routes_turns).reshape((SEQ, TOP))
    probs = jnp.clip(0.049804688 + 0.9501953 * jax.random.uniform(keys[7], (SEQ, TOP), jnp.float32) ** levels(keys[7], (SEQ, TOP), ((0, 32),), -0.2, 0.2), 0.049804688, 1.0).astype(jnp.bfloat16)
    w_gate = centred(keys[8], (EXPERTS, D, FFN), D ** -0.5, 0.0625, ((0, 32), (1, 8)))
    w_up = centred(keys[9], (EXPERTS, D, FFN), D ** -0.5, 0.0625, ((0, 32), (1, 8)))
    w_down = centred(keys[10], (EXPERTS, FFN, D), FFN ** -0.5, 0.1875, ((0, 32), (2, 8)))
    return {"logits": logits, "head_weight": head_weight, "token_ids": token_ids, "slab_order": slab_order, "token_weights": token_weights, "moe_input": moe_input, "routes": routes, "probs": probs, "w_gate": w_gate, "w_up": w_up, "w_down": w_down}


def reference(logits, head_weight, token_ids, slab_order, token_weights, moe_input, routes, probs, w_gate, w_up, w_down):
    seq_rows = jnp.arange(SEQ, dtype=jnp.int32)
    position = (slab_order[seq_rows // SLAB] * SLAB + seq_rows % SLAB).astype(jnp.int32)
    has_target = position < SEQ - 1
    target = token_ids[jnp.minimum(position + 1, SEQ - 1)]
    weighting = jnp.where(has_target, token_weights, jnp.zeros_like(token_weights))
    scores = logits.astype(jnp.float32)
    row_max = jnp.max(scores, axis=1)
    shifted = jnp.exp(scores - row_max[:, None])
    row_total = jnp.sum(shifted, axis=1)
    is_target = jnp.arange(VOCAB, dtype=jnp.int32)[None, :] == target[:, None]
    logit_grads = (weighting[:, None] * (shifted / row_total[:, None] - is_target.astype(jnp.float32))).astype(jnp.bfloat16)
    upstream = jnp.dot(logit_grads, head_weight, preferred_element_type=jnp.float32)
    upstream_sent = upstream.astype(jnp.bfloat16)
    route_list = routes.reshape(-1)
    prob_list = probs.reshape(-1).astype(jnp.float32)
    slot_limit = N_EXP * CAP

    def expert_step(state_pair, expert):
        accum, prob_accum = state_pair
        picked = jnp.argsort((route_list != expert).astype(jnp.int32), stable=True)[:slot_limit].astype(jnp.int32)
        is_live = route_list[picked] == expert
        source_row = (picked // TOP).astype(jnp.int32)
        slot_inputs = moe_input[source_row]
        slot_upstream = upstream_sent[source_row]
        slot_prob = jnp.where(is_live, prob_list[picked], jnp.zeros_like(prob_list[picked]))
        gate_w = w_gate[expert]
        up_w = w_up[expert]
        down_w = w_down[expert]
        gate_pre = jnp.dot(slot_inputs, gate_w, preferred_element_type=jnp.float32)
        up_pre = jnp.dot(slot_inputs, up_w, preferred_element_type=jnp.float32)
        back_pre = jnp.dot(slot_upstream, down_w.T, preferred_element_type=jnp.float32)
        gate_sigmoid = jax.nn.sigmoid(gate_pre)
        gate_silu = gate_pre * gate_sigmoid
        slot_prob_grad = jnp.sum(gate_silu * up_pre * back_pre, axis=1)
        scaled_back = slot_prob[:, None] * back_pre
        gate_grad = (scaled_back * up_pre * gate_sigmoid * (1.0 + gate_pre * (1.0 - gate_sigmoid))).astype(jnp.bfloat16)
        up_grad = (scaled_back * gate_silu).astype(jnp.bfloat16)
        slot_grad = (jnp.dot(gate_grad, gate_w.T, preferred_element_type=jnp.float32)
                     + jnp.dot(up_grad, up_w.T, preferred_element_type=jnp.float32))
        accum = accum.at[source_row].add(jnp.where(is_live[:, None], slot_grad, jnp.zeros((), jnp.float32)))
        prob_accum = prob_accum.at[picked].add(jnp.where(is_live, slot_prob_grad, jnp.zeros((), jnp.float32)))
        return (accum, prob_accum), None

    start_state = (jnp.zeros((SEQ, D), jnp.float32), jnp.zeros((SEQ * TOP,), jnp.float32))
    (accum, prob_accum), unused = lax.scan(expert_step, start_state, jnp.arange(EXPERTS, dtype=jnp.int32))
    d_x = upstream + accum
    d_prob = prob_accum.reshape(SEQ, TOP)
    return d_x, d_prob
```

```python
import jax
import jax.numpy as jnp
from jax import lax
from jax.sharding import PartitionSpec as P

SLAB = 64
NY, NZ = 4, 8
Y_GROUPS = [[y * NZ + z for y in range(NY)] for z in range(NZ)]
Z_GROUPS = [[y * NZ + z for z in range(NZ)] for y in range(NY)]
PAIR_GROUPS = [[2 * c, 2 * c + 1] for c in range(4)]
X_GROUPS = [[2 * c + p for c in range(4)] for p in range(2)]
CONTRACT_LAST = (((1,), (1,)), ((), ()))


def exchange(x, axis, groups=None):
    return lax.all_to_all(x, axis, 0, 0, tiled=True, axis_index_groups=groups)


def exchange_sum(x, axis, groups, parts):
    rows, width = x.shape
    got = exchange(x, axis, groups).reshape(parts, rows // parts, width)
    return jnp.sum(got.astype(jnp.float32), axis=0)


def sum_over_ctx(x):
    half = exchange_sum(x.astype(jnp.float16), "ctx", PAIR_GROUPS, 2).astype(jnp.float16)
    own = exchange_sum(half, "ctx", X_GROUPS, 4).astype(jnp.float16)
    rows, width = own.shape
    spread = jnp.broadcast_to(own[None], (4, rows, width)).reshape(4 * rows, width)
    half = exchange(spread, "ctx", X_GROUPS)
    other = lax.ppermute(half, "ctx", [(i, i ^ 1) for i in range(8)])
    core = lax.axis_index("ctx") % 2
    first = jnp.where(core == 0, half, other)
    second = jnp.where(core == 0, other, half)
    return jnp.concatenate([first, second], axis=0).astype(jnp.float32)


def unit_backward(gate_sum, up_sum, back_sum, slot_prob):
    gate_sigmoid = jax.nn.sigmoid(gate_sum)
    gate_silu = gate_sum * gate_sigmoid
    prob_part = jnp.sum(gate_silu * up_sum * back_sum, axis=1)
    scaled_back = slot_prob[:, None] * back_sum
    gate_grad = (
        scaled_back * up_sum * gate_sigmoid * (1.0 + gate_sum * (1.0 - gate_sigmoid))
    ).astype(jnp.bfloat16)
    up_grad = (scaled_back * gate_silu).astype(jnp.bfloat16)
    return (gate_grad, up_grad, prob_part)


def local(
    logits,
    head_weight,
    token_ids,
    slab_order,
    token_weights,
    moe_input,
    routes,
    probs,
    w_gate,
    w_up,
    w_down,
):
    ctx_count = lax.axis_size("ctx")
    exp_count = lax.axis_size("exp")
    row_count, vocab_width = logits.shape
    seq_length = row_count * ctx_count
    all_logits = lax.all_gather(logits, "ctx", axis=0, tiled=True)

    token_count, route_count = routes.shape
    feature_width = moe_input.shape[1]
    capacity = min(token_count, 2 * token_count * route_count // exp_count)
    slot_count = exp_count * capacity
    route_list = routes.reshape(-1)
    expert_match = (route_list[:, None] == jnp.arange(exp_count, dtype=jnp.int32)[None, :]).astype(
        jnp.int32
    )
    route_rank = jnp.sum((jnp.cumsum(expert_match, axis=0) - 1) * expert_match, axis=1)
    slot_of_route = route_list * capacity + route_rank
    chosen = (jnp.arange(slot_count, dtype=jnp.int32)[:, None] == slot_of_route[None, :]).astype(
        jnp.float32
    )
    slot_owner = jnp.sum(chosen.reshape(slot_count, token_count, route_count), axis=2).astype(
        jnp.bfloat16
    )

    scores = logits.astype(jnp.float32)
    local_max = jnp.max(scores, axis=1)
    local_sum = jnp.sum(jnp.exp(scores - local_max[:, None]), axis=1)
    send_prob = jnp.dot(
        chosen, probs.reshape(-1).astype(jnp.float32), precision=lax.Precision.HIGHEST
    ).reshape(exp_count, capacity)
    packed = jnp.concatenate(
        [
            jnp.broadcast_to(local_max[None], (exp_count, row_count)),
            jnp.broadcast_to(local_sum[None], (exp_count, row_count)),
            jnp.pad(send_prob, ((0, 0), (0, 128 - capacity))),
        ],
        axis=1,
    )
    packed = exchange(packed, "exp")
    all_max = packed[:, :row_count]
    row_max = jnp.max(all_max, axis=0)
    row_total = jnp.sum(packed[:, row_count : 2 * row_count] * jnp.exp(all_max - row_max), axis=0)
    flat_prob = packed[:, 2 * row_count : 2 * row_count + capacity].reshape(-1)
    rows = jnp.stack([row_max, row_total, token_weights, token_ids.astype(jnp.float32)])
    rows = lax.all_gather(rows, "ctx", axis=1, tiled=True)
    row_max, row_total, weights = rows[0], rows[1], rows[2]
    all_ids = rows[3].astype(jnp.int32)

    send_input = jnp.dot(slot_owner, moe_input, preferred_element_type=jnp.float32).astype(
        jnp.bfloat16
    )
    flat_inputs = exchange(send_input, "exp")
    gate_w = w_gate[0]
    up_w = w_up[0]
    down_w = w_down[0]
    part_gate = jnp.dot(flat_inputs, gate_w, preferred_element_type=jnp.float32)
    part_up = jnp.dot(flat_inputs, up_w, preferred_element_type=jnp.float32)
    gate_sum, up_sum = lax.psum((part_gate, part_up), "ctx")

    storage = jnp.arange(seq_length, dtype=jnp.int32)
    slab_match = (
        jnp.arange(slab_order.shape[0], dtype=jnp.int32)[None, :] == (storage // SLAB)[:, None]
    )
    placed_slab = jnp.sum(jnp.where(slab_match, slab_order[None, :], 0), axis=1)
    position = placed_slab * SLAB + storage % SLAB
    has_target = position < seq_length - 1
    target = jnp.take(all_ids, jnp.minimum(position + 1, seq_length - 1))
    local_target = target - lax.axis_index("exp") * vocab_width
    weighting = jnp.where(has_target, weights, 0.0)
    is_target = jnp.arange(vocab_width, dtype=jnp.int32)[None, :] == local_target[:, None]
    logit_grads = (
        weighting[:, None]
        * (
            jnp.exp(all_logits.astype(jnp.float32) - row_max[:, None]) / row_total[:, None]
            - is_target.astype(jnp.float32)
        )
    ).astype(jnp.bfloat16)
    partial = jnp.dot(logit_grads, head_weight, preferred_element_type=jnp.float32)
    over_y = exchange_sum((partial * 4096.0).astype(jnp.float16), "exp", Y_GROUPS, NY)
    upstream = exchange_sum(over_y.astype(jnp.float16), "exp", Z_GROUPS, NZ) * (1.0 / 4096.0)
    upstream_sent = upstream.astype(jnp.bfloat16)

    send_upstream = jnp.dot(slot_owner, upstream_sent, preferred_element_type=jnp.float32).astype(
        jnp.bfloat16
    )
    flat_upstream = exchange(send_upstream, "exp")
    part_back = lax.dot_general(
        flat_upstream, down_w, CONTRACT_LAST, preferred_element_type=jnp.float32
    )
    back_sum = sum_over_ctx(part_back)
    gate_grad, up_grad, prob_grad = unit_backward(gate_sum, up_sum, back_sum, flat_prob)
    input_grad = lax.dot_general(
        gate_grad, gate_w, CONTRACT_LAST, preferred_element_type=jnp.float32
    ) + lax.dot_general(up_grad, up_w, CONTRACT_LAST, preferred_element_type=jnp.float32)
    prob_high = lax.reduce_precision(prob_grad, 8, 7)
    prob_low = prob_grad - prob_high
    lane = jnp.arange(128, dtype=jnp.int32)[None, :]
    prob_block = jnp.where(
        lane == 0, prob_high[:, None], jnp.where(lane == 1, prob_low[:, None], 0)
    ).astype(jnp.bfloat16)
    back = exchange(
        jnp.concatenate([input_grad.astype(jnp.bfloat16), prob_block], axis=1), "exp"
    )
    back_input = back[:, :feature_width]
    back_prob = back[:, feature_width].astype(jnp.float32) + back[:, feature_width + 1].astype(
        jnp.float32
    )
    d_x = upstream + lax.dot_general(
        slot_owner, back_input, (((0,), (0,)), ((), ())), preferred_element_type=jnp.float32
    )
    d_prob = jnp.dot(back_prob, chosen, precision=lax.Precision.HIGHEST).reshape(
        token_count, route_count
    )
    return (d_x, d_prob)


def solution(mesh):
    placed = (
        P("ctx", "exp"),
        P("exp", "ctx"),
        P("ctx"),
        P(),
        P("ctx"),
        P("exp", "ctx"),
        P("exp", None),
        P("exp", None),
        P("exp", "ctx", None),
        P("exp", "ctx", None),
        P("exp", None, "ctx"),
    )
    return jax.shard_map(
        local,
        mesh=mesh,
        in_specs=placed,
        out_specs=(P("exp", "ctx"), P("exp", None)),
        check_vma=False,
    )
```

```python
import jax
import jax.numpy as jnp
from jax import lax
from jax.sharding import PartitionSpec as P

SLAB = 64
NY, NZ = 4, 8
Z_GROUPS = [[y * NZ + z for z in range(NZ)] for y in range(NY)]
CONTRACT_LAST = (((1,), (1,)), ((), ()))


def exchange(x, axis, groups=None):
    return lax.all_to_all(x, axis, 0, 0, tiled=True, axis_index_groups=groups)


def exchange_sum(x, axis, groups, parts):
    rows, width = x.shape
    got = exchange(x, axis, groups).reshape(parts, rows // parts, width)
    return jnp.sum(got.astype(jnp.float32), axis=0)


def split_high(x):
    high = lax.reduce_precision(x, 8, 7)
    return high, x - high


def ctx_shift(x, shift):
    return lax.ppermute(x, "ctx", [(i, (i + 2 * shift) % 8) for i in range(8)])


def ctx_swap(x):
    return lax.ppermute(x, "ctx", [(i, i ^ 1) for i in range(8)])


def rows_at(x, index, count):
    return lax.dynamic_slice_in_dim(x, index * count, count, axis=0)


def sum_over_ctx(x):
    core = lax.axis_index("ctx") % 2
    chip = lax.axis_index("ctx") // 2
    half_rows = x.shape[0] // 2
    own_rows = half_rows // 4
    x = x.astype(jnp.float16)
    other = ctx_swap(rows_at(x, 1 - core, half_rows))
    pair = (
        rows_at(x, core, half_rows).astype(jnp.float32) + other.astype(jnp.float32)
    ).astype(jnp.float16)
    got = [ctx_shift(rows_at(pair, (chip + shift) % 4, own_rows), shift) for shift in (1, 3, 2)]
    own = rows_at(pair, chip, own_rows).astype(jnp.float32)
    for piece in got:
        own = own + piece.astype(jnp.float32)
    own = own.astype(jnp.float16)
    from_one, from_three, from_two = [ctx_shift(own, shift) for shift in (1, 3, 2)]
    half = jnp.zeros((half_rows, x.shape[1]), jnp.float16)
    for piece, shift in ((own, 0), (from_one, 1), (from_three, 3), (from_two, 2)):
        half = lax.dynamic_update_slice_in_dim(half, piece, (chip + 4 - shift) % 4 * own_rows, axis=0)
    other = ctx_swap(half)
    first = jnp.where(core == 0, half, other).astype(jnp.float32)
    second = jnp.where(core == 0, other, half).astype(jnp.float32)
    return jnp.concatenate([first, second], axis=0)


def y_shift(x, shift):
    return lax.ppermute(
        x, "exp", [(i, (i + NZ * shift) % (NY * NZ)) for i in range(NY * NZ)]
    )


def ring_sum_over_y(x):
    y = lax.axis_index("exp") // NZ
    count = x.shape[0] // NY
    split = 512
    far = rows_at(x, (y + 2) % NY, count)
    up = rows_at(x, (y + 1) % NY, count)
    down = rows_at(x, (y + 3) % NY, count)
    from_down = y_shift(far[:, :split], 1)
    from_up = y_shift(far[:, split:], 3)
    up_sum = (up[:, :split].astype(jnp.float32) + from_down.astype(jnp.float32)).astype(x.dtype)
    down_sum = (down[:, split:].astype(jnp.float32) + from_up.astype(jnp.float32)).astype(x.dtype)
    up_late = y_shift(up[:, split:], 1)
    down_late = y_shift(down[:, :split], 3)
    up_sum = y_shift(up_sum, 1)
    down_sum = y_shift(down_sum, 3)
    own = rows_at(x, y, count).astype(jnp.float32)
    left = own[:, :split] + up_sum.astype(jnp.float32) + down_late.astype(jnp.float32)
    right = own[:, split:] + up_late.astype(jnp.float32) + down_sum.astype(jnp.float32)
    return jnp.concatenate([left, right], axis=1)


def unit_backward(gate_sum, up_sum, back_sum, slot_prob):
    gate_sigmoid = jax.nn.sigmoid(gate_sum)
    gate_silu = gate_sum * gate_sigmoid
    prob_part = jnp.sum(gate_silu * up_sum * back_sum, axis=1)
    scaled_back = slot_prob[:, None] * back_sum
    gate_grad = (
        scaled_back * up_sum * gate_sigmoid * (1.0 + gate_sum * (1.0 - gate_sigmoid))
    ).astype(jnp.bfloat16)
    up_grad = (scaled_back * gate_silu).astype(jnp.bfloat16)
    return (gate_grad, up_grad, prob_part)


def local(
    logits,
    head_weight,
    token_ids,
    slab_order,
    token_weights,
    moe_input,
    routes,
    probs,
    w_gate,
    w_up,
    w_down,
):
    ctx_count = lax.axis_size("ctx")
    exp_count = lax.axis_size("exp")
    row_count, vocab_width = logits.shape
    seq_length = row_count * ctx_count
    all_logits = lax.all_gather(logits, "ctx", axis=0, tiled=True)

    token_count, route_count = routes.shape
    feature_width = moe_input.shape[1]
    capacity = min(token_count, 2 * token_count * route_count // exp_count)
    slot_count = exp_count * capacity
    route_list = routes.reshape(-1)
    expert_match = (route_list[:, None] == jnp.arange(exp_count, dtype=jnp.int32)[None, :]).astype(
        jnp.int32
    )
    route_rank = jnp.sum((jnp.cumsum(expert_match, axis=0) - 1) * expert_match, axis=1)
    slot_of_route = route_list * capacity + route_rank
    chosen = (jnp.arange(slot_count, dtype=jnp.int32)[:, None] == slot_of_route[None, :]).astype(
        jnp.float32
    )
    slot_owner = jnp.sum(chosen.reshape(slot_count, token_count, route_count), axis=2).astype(
        jnp.bfloat16
    )

    scores = logits.astype(jnp.float32)
    local_max = jnp.max(scores, axis=1)
    local_sum = jnp.sum(jnp.exp(scores - local_max[:, None]), axis=1)
    send_prob = jnp.dot(
        chosen, probs.reshape(-1).astype(jnp.float32), precision=lax.Precision.HIGHEST
    ).reshape(exp_count, capacity)
    send_input = jnp.dot(slot_owner, moe_input, preferred_element_type=jnp.float32).astype(
        jnp.bfloat16
    )
    packed = jnp.concatenate(
        [
            jnp.broadcast_to(local_max[None], (exp_count, row_count)),
            jnp.broadcast_to(local_sum[None], (exp_count, row_count)),
            jnp.pad(send_prob, ((0, 0), (0, 128 - capacity))),
        ],
        axis=1,
    )
    packed = exchange(packed, "exp")
    all_max = packed[:, :row_count]
    row_max = jnp.max(all_max, axis=0)
    row_total = jnp.sum(packed[:, row_count : 2 * row_count] * jnp.exp(all_max - row_max), axis=0)
    flat_prob = packed[:, 2 * row_count : 2 * row_count + capacity].reshape(-1)
    rows = jnp.concatenate([row_max, row_total, token_weights, token_ids.astype(jnp.float32)])
    rows = exchange(jnp.broadcast_to(rows[None], (ctx_count, 4 * row_count)), "ctx")
    rows = rows.reshape(ctx_count, 4, row_count).transpose(1, 0, 2).reshape(4, seq_length)
    rows, send_input, all_logits = lax.optimization_barrier((rows, send_input, all_logits))
    flat_inputs = exchange(send_input, "exp")

    gate_w = w_gate[0]
    up_w = w_up[0]
    down_w = w_down[0]
    part_gate = jnp.dot(flat_inputs, gate_w, preferred_element_type=jnp.float32)
    part_up = jnp.dot(flat_inputs, up_w, preferred_element_type=jnp.float32)
    part_both = jnp.concatenate(
        [part_gate.astype(jnp.float16), part_up.astype(jnp.float16)], axis=1
    )
    both_sum = sum_over_ctx(part_both)
    row_max, row_total, weights = rows[0], rows[1], rows[2]
    all_ids = rows[3].astype(jnp.int32)

    slab_count = slab_order.shape[0]
    next_ids = jnp.concatenate([all_ids[1:], all_ids[-1:]]).reshape(slab_count, SLAB)
    slab_match = slab_order[:, None] == jnp.arange(slab_count, dtype=jnp.int32)[None, :]
    target = jnp.sum(jnp.where(slab_match[:, :, None], next_ids[None], 0), axis=1).reshape(-1)
    position = (slab_order[:, None] * SLAB + jnp.arange(SLAB, dtype=jnp.int32)).reshape(-1)
    has_target = position < seq_length - 1
    local_target = target - lax.axis_index("exp") * vocab_width
    weighting = jnp.where(has_target, weights, 0.0)
    is_target = jnp.arange(vocab_width, dtype=jnp.int32)[None, :] == local_target[:, None]
    logit_grads = (
        weighting[:, None]
        * (
            jnp.exp(all_logits.astype(jnp.float32) - row_max[:, None]) / row_total[:, None]
            - is_target.astype(jnp.float32)
        )
    ).astype(jnp.bfloat16)
    partial = jnp.dot(logit_grads, head_weight, preferred_element_type=jnp.float32)
    over_y = ring_sum_over_y((partial * 4096.0).astype(jnp.float16))
    upstream = exchange_sum(over_y.astype(jnp.float16), "exp", Z_GROUPS, NZ) * (1.0 / 4096.0)
    upstream_sent = upstream.astype(jnp.bfloat16)

    send_upstream = jnp.dot(slot_owner, upstream_sent, preferred_element_type=jnp.float32).astype(
        jnp.bfloat16
    )
    flat_upstream = exchange(send_upstream, "exp")
    flat_upstream, both_sum = lax.optimization_barrier((flat_upstream, both_sum))
    gate_sum = both_sum[:, : gate_w.shape[1]]
    up_sum = both_sum[:, gate_w.shape[1] :]
    part_back = lax.dot_general(
        flat_upstream, down_w, CONTRACT_LAST, preferred_element_type=jnp.float32
    )
    back_sum = sum_over_ctx(part_back)
    gate_grad, up_grad, prob_grad = unit_backward(gate_sum, up_sum, back_sum, flat_prob)
    input_grad = lax.dot_general(
        gate_grad, gate_w, CONTRACT_LAST, preferred_element_type=jnp.float32
    ) + lax.dot_general(up_grad, up_w, CONTRACT_LAST, preferred_element_type=jnp.float32)
    prob_high, prob_low = split_high(prob_grad)
    lane = jnp.arange(128, dtype=jnp.int32)[None, :]
    prob_block = jnp.where(
        lane == 0, prob_high[:, None], jnp.where(lane == 1, prob_low[:, None], 0)
    ).astype(jnp.bfloat16)
    back = exchange(
        jnp.concatenate([input_grad.astype(jnp.bfloat16), prob_block], axis=1), "exp"
    )
    back_input = back[:, :feature_width]
    back_prob = back[:, feature_width].astype(jnp.float32) + back[:, feature_width + 1].astype(
        jnp.float32
    )
    d_x = upstream + lax.dot_general(
        slot_owner, back_input, (((0,), (0,)), ((), ())), preferred_element_type=jnp.float32
    )
    d_prob = jnp.dot(back_prob, chosen, precision=lax.Precision.HIGHEST).reshape(
        token_count, route_count
    )
    return (d_x, d_prob)


def solution(mesh):
    placed = (
        P("ctx", "exp"),
        P("exp", "ctx"),
        P("ctx"),
        P(),
        P("ctx"),
        P("exp", "ctx"),
        P("exp", None),
        P("exp", None),
        P("exp", "ctx", None),
        P("exp", "ctx", None),
        P("exp", None, "ctx"),
    )
    return jax.shard_map(
        local,
        mesh=mesh,
        in_specs=placed,
        out_specs=(P("exp", "ctx"), P("exp", None)),
        check_vma=False,
    )
```

```python
import jax
import jax.numpy as jnp
from jax import lax
from jax.sharding import PartitionSpec as P

SLAB = 64
NY, NZ = 4, 8
Z_GROUPS = [[y * NZ + z for z in range(NZ)] for y in range(NY)]
CONTRACT_LAST = (((1,), (1,)), ((), ()))


def exchange(x, axis, groups=None):
    return lax.all_to_all(x, axis, 0, 0, tiled=True, axis_index_groups=groups)


def exchange_sum(x, axis, groups, parts):
    rows, width = x.shape
    got = exchange(x, axis, groups).reshape(parts, rows // parts, width)
    return jnp.sum(got.astype(jnp.float32), axis=0)


def split_high(x):
    high = lax.reduce_precision(x, 8, 7)
    return high, x - high


def halves_first(x, groups):
    rows, width = x.shape
    x = x.reshape(groups, 2, rows // groups // 2, width)
    return x.transpose(1, 0, 2, 3).reshape(rows, width)


def ctx_shift(x, shift):
    return lax.ppermute(x, "ctx", [(i, (i + 2 * shift) % 8) for i in range(8)])


def ctx_swap(x):
    return lax.ppermute(x, "ctx", [(i, i ^ 1) for i in range(8)])


def rows_at(x, index, count):
    return lax.dynamic_slice_in_dim(x, index * count, count, axis=0)


def ctx_scatter(x):
    core = lax.axis_index("ctx") % 2
    chip = lax.axis_index("ctx") // 2
    half_rows = x.shape[0] // 2
    own_rows = half_rows // 4
    x = x.astype(jnp.float16)
    other = ctx_swap(rows_at(x, 1 - core, half_rows))
    pair = (
        rows_at(x, core, half_rows).astype(jnp.float32) + other.astype(jnp.float32)
    ).astype(jnp.float16)
    got = [ctx_shift(rows_at(pair, (chip + shift) % 4, own_rows), shift) for shift in (1, 3, 2)]
    own = rows_at(pair, chip, own_rows).astype(jnp.float32)
    for piece in got:
        own = own + piece.astype(jnp.float32)
    return own.astype(jnp.float16)


def ctx_gather(own):
    core = lax.axis_index("ctx") % 2
    chip = lax.axis_index("ctx") // 2
    own_rows, width = own.shape
    from_one, from_three, from_two = [ctx_shift(own, shift) for shift in (1, 3, 2)]
    half = jnp.zeros((4 * own_rows, width), jnp.float16)
    for piece, shift in ((own, 0), (from_one, 1), (from_three, 3), (from_two, 2)):
        half = lax.dynamic_update_slice_in_dim(half, piece, (chip + 4 - shift) % 4 * own_rows, axis=0)
    other = ctx_swap(half)
    first = jnp.where(core == 0, half, other).astype(jnp.float32)
    second = jnp.where(core == 0, other, half).astype(jnp.float32)
    return jnp.concatenate([first, second], axis=0)


def y_shift(x, shift):
    return lax.ppermute(
        x, "exp", [(i, (i + NZ * shift) % (NY * NZ)) for i in range(NY * NZ)]
    )


def ring_sum_over_y(block):
    y = lax.axis_index("exp") // NZ
    split = 512
    far = block((y + 2) % NY)
    from_down = y_shift(far[:, :split], 1)
    from_up = y_shift(far[:, split:], 3)
    up = block((y + 1) % NY)
    up_late = y_shift(up[:, split:], 1)
    down = block((y + 3) % NY)
    down_late = y_shift(down[:, :split], 3)
    up_sum = (up[:, :split].astype(jnp.float32) + from_down.astype(jnp.float32)).astype(up.dtype)
    up_sum = y_shift(up_sum, 1)
    down_sum = (down[:, split:].astype(jnp.float32) + from_up.astype(jnp.float32)).astype(up.dtype)
    down_sum = y_shift(down_sum, 3)
    own = block(y).astype(jnp.float32)
    left = own[:, :split] + up_sum.astype(jnp.float32) + down_late.astype(jnp.float32)
    right = own[:, split:] + up_late.astype(jnp.float32) + down_sum.astype(jnp.float32)
    return jnp.concatenate([left, right], axis=1).astype(up.dtype)


def unit_backward(gate_sum, up_sum, back_sum, slot_prob):
    gate_sigmoid = jax.nn.sigmoid(gate_sum)
    gate_silu = gate_sum * gate_sigmoid
    prob_part = jnp.sum(gate_silu * up_sum * back_sum, axis=1)
    scaled_back = slot_prob[:, None] * back_sum
    gate_grad = (
        scaled_back * up_sum * gate_sigmoid * (1.0 + gate_sum * (1.0 - gate_sigmoid))
    ).astype(jnp.bfloat16)
    up_grad = (scaled_back * gate_silu).astype(jnp.bfloat16)
    return (gate_grad, up_grad, prob_part)


def local(
    logits,
    head_weight,
    token_ids,
    slab_order,
    token_weights,
    moe_input,
    routes,
    probs,
    w_gate,
    w_up,
    w_down,
):
    ctx_count = lax.axis_size("ctx")
    exp_count = lax.axis_size("exp")
    row_count, vocab_width = logits.shape
    seq_length = row_count * ctx_count
    all_logits = lax.all_gather(logits, "ctx", axis=0, tiled=True)

    token_count, route_count = routes.shape
    feature_width = moe_input.shape[1]
    capacity = min(token_count, 2 * token_count * route_count // exp_count)
    slot_count = exp_count * capacity
    route_list = routes.reshape(-1)
    expert_match = (route_list[:, None] == jnp.arange(exp_count, dtype=jnp.int32)[None, :]).astype(
        jnp.int32
    )
    route_rank = jnp.sum((jnp.cumsum(expert_match, axis=0) - 1) * expert_match, axis=1)
    slot_of_route = route_list * capacity + route_rank
    chosen = (jnp.arange(slot_count, dtype=jnp.int32)[:, None] == slot_of_route[None, :]).astype(
        jnp.float32
    )
    slot_owner = jnp.sum(chosen.reshape(slot_count, token_count, route_count), axis=2).astype(
        jnp.bfloat16
    )
    half_owner = jnp.split(halves_first(slot_owner, exp_count), 2)

    scores = logits.astype(jnp.float32)
    local_max = jnp.max(scores, axis=1)
    local_sum = jnp.sum(jnp.exp(scores - local_max[:, None]), axis=1)
    send_prob = jnp.dot(
        chosen, probs.reshape(-1).astype(jnp.float32), precision=lax.Precision.HIGHEST
    ).reshape(exp_count, capacity)
    send_input = jnp.dot(slot_owner, moe_input, preferred_element_type=jnp.float32).astype(
        jnp.bfloat16
    )
    packed = jnp.concatenate(
        [
            jnp.broadcast_to(local_max[None], (exp_count, row_count)),
            jnp.broadcast_to(local_sum[None], (exp_count, row_count)),
            jnp.pad(send_prob, ((0, 0), (0, 128 - capacity))),
        ],
        axis=1,
    )
    packed = exchange(packed, "exp")
    all_max = packed[:, :row_count]
    row_max = jnp.max(all_max, axis=0)
    row_total = jnp.sum(packed[:, row_count : 2 * row_count] * jnp.exp(all_max - row_max), axis=0)
    flat_prob = halves_first(
        packed[:, 2 * row_count : 2 * row_count + capacity].reshape(slot_count, 1), exp_count
    ).reshape(-1)
    rows = jnp.concatenate([row_max, row_total, token_weights, token_ids.astype(jnp.float32)])
    rows = exchange(jnp.broadcast_to(rows[None], (ctx_count, 4 * row_count)), "ctx")
    rows = rows.reshape(ctx_count, 4, row_count).transpose(1, 0, 2).reshape(4, seq_length)
    rows, send_input = lax.optimization_barrier((rows, send_input))
    flat_inputs = halves_first(exchange(send_input, "exp"), exp_count)
    rows, all_logits = lax.optimization_barrier((rows, all_logits))

    gate_w = w_gate[0]
    up_w = w_up[0]
    down_w = w_down[0]
    row_max, row_total, weights = rows[0], rows[1], rows[2]
    all_ids = rows[3].astype(jnp.int32)

    slab_count = slab_order.shape[0]
    next_ids = jnp.concatenate([all_ids[1:], all_ids[-1:]]).reshape(slab_count, SLAB)
    slab_match = slab_order[:, None] == jnp.arange(slab_count, dtype=jnp.int32)[None, :]
    target = jnp.sum(jnp.where(slab_match[:, :, None], next_ids[None], 0), axis=1).reshape(-1)
    position = (slab_order[:, None] * SLAB + jnp.arange(SLAB, dtype=jnp.int32)).reshape(-1)
    has_target = position < seq_length - 1
    local_target = target - lax.axis_index("exp") * vocab_width
    weighting = jnp.where(has_target, weights, 0.0)
    columns = jnp.arange(vocab_width, dtype=jnp.int32)[None, :]
    per_row = jnp.stack([row_max, row_total, weighting, local_target.astype(jnp.float32)])

    def upstream_block(q):
        count = seq_length // NY
        top, total, weight, aim = lax.dynamic_slice_in_dim(per_row, q * count, count, axis=1)
        is_target = columns == aim.astype(jnp.int32)[:, None]
        logit_grads = (
            weight[:, None]
            * (
                jnp.exp(rows_at(all_logits, q, count).astype(jnp.float32) - top[:, None])
                / total[:, None]
                - is_target.astype(jnp.float32)
            )
        ).astype(jnp.bfloat16)
        partial = jnp.dot(logit_grads, head_weight, preferred_element_type=jnp.float32)
        return (partial * 4096.0).astype(jnp.float16)

    over_y = ring_sum_over_y(upstream_block)
    flat_inputs, over_y = lax.optimization_barrier((flat_inputs, over_y))
    part_gate = jnp.dot(flat_inputs, gate_w, preferred_element_type=jnp.float32)
    part_up = jnp.dot(flat_inputs, up_w, preferred_element_type=jnp.float32)
    part_both = jnp.concatenate(
        [part_gate.astype(jnp.float16), part_up.astype(jnp.float16)], axis=1
    )
    over_y, part_both = lax.optimization_barrier((over_y, part_both))
    upstream = exchange_sum(over_y, "exp", Z_GROUPS, NZ) * (1.0 / 4096.0)
    upstream_sent = upstream.astype(jnp.bfloat16)

    send_upstream = [
        jnp.dot(owner, upstream_sent, preferred_element_type=jnp.float32).astype(jnp.bfloat16)
        for owner in half_owner
    ]
    both_own, send_upstream[0] = lax.optimization_barrier((ctx_scatter(part_both), send_upstream[0]))
    both_sum = ctx_gather(both_own)

    def back_part(flat):
        return lax.dot_general(flat, down_w, CONTRACT_LAST, preferred_element_type=jnp.float32)

    hidden = gate_w.shape[1]
    half_slots = slot_count // 2
    lane = jnp.arange(128, dtype=jnp.int32)[None, :]

    def route_gradients(half, back_sum):
        rows_of = slice(half * half_slots, (half + 1) * half_slots)
        both = both_sum[rows_of]
        gate_grad, up_grad, prob_grad = unit_backward(
            both[:, :hidden], both[:, hidden:], back_sum, flat_prob[rows_of]
        )
        input_grad = lax.dot_general(
            gate_grad, gate_w, CONTRACT_LAST, preferred_element_type=jnp.float32
        ) + lax.dot_general(up_grad, up_w, CONTRACT_LAST, preferred_element_type=jnp.float32)
        prob_high, prob_low = split_high(prob_grad)
        prob_block = jnp.where(
            lane == 0, prob_high[:, None], jnp.where(lane == 1, prob_low[:, None], 0)
        ).astype(jnp.bfloat16)
        return jnp.concatenate([input_grad.astype(jnp.bfloat16), prob_block], axis=1)

    barrier = lax.optimization_barrier
    flat_first = exchange(send_upstream[0], "exp")
    send_upstream[1], flat_first = barrier((send_upstream[1], flat_first))
    flat_second = exchange(send_upstream[1], "exp")
    own_first = ctx_scatter(back_part(flat_first))
    flat_second, own_first, both_sum = barrier((flat_second, own_first, both_sum))
    back_first = ctx_gather(own_first)
    own_second = ctx_scatter(back_part(flat_second))
    back_first, own_second = barrier((back_first, own_second))
    send_first = route_gradients(0, back_first)
    send_first, own_second = barrier((send_first, own_second))
    got_first = exchange(send_first, "exp")
    send_second = route_gradients(1, ctx_gather(own_second))
    send_second, got_first = barrier((send_second, got_first))
    got_second = exchange(send_second, "exp")

    d_x = upstream
    back_prob = []
    for owner, got in zip(half_owner, (got_first, got_second)):
        d_x = d_x + lax.dot_general(
            owner,
            got[:, :feature_width],
            (((0,), (0,)), ((), ())),
            preferred_element_type=jnp.float32,
        )
        back_prob.append(
            got[:, feature_width].astype(jnp.float32)
            + got[:, feature_width + 1].astype(jnp.float32)
        )
    back_prob = jnp.concatenate(
        [part.reshape(exp_count, capacity // 2) for part in back_prob], axis=1
    ).reshape(-1)
    d_prob = jnp.dot(back_prob, chosen, precision=lax.Precision.HIGHEST).reshape(
        token_count, route_count
    )
    return (d_x, d_prob)


def solution(mesh):
    placed = (
        P("ctx", "exp"),
        P("exp", "ctx"),
        P("ctx"),
        P(),
        P("ctx"),
        P("exp", "ctx"),
        P("exp", None),
        P("exp", None),
        P("exp", "ctx", None),
        P("exp", "ctx", None),
        P("exp", None, "ctx"),
    )
    return jax.shard_map(
        local,
        mesh=mesh,
        in_specs=placed,
        out_specs=(P("exp", "ctx"), P("exp", None)),
        check_vma=False,
    )
```

```python
import jax
import jax.numpy as jnp
from jax import lax
from jax.sharding import PartitionSpec as P

SLAB = 64
NY, NZ = 4, 8
Z_GROUPS = [[y * NZ + z for z in range(NZ)] for y in range(NY)]
CONTRACT_LAST = (((1,), (1,)), ((), ()))


def exchange(x, axis, groups=None):
    return lax.all_to_all(x, axis, 0, 0, tiled=True, axis_index_groups=groups)


def exchange_sum(x, axis, groups, parts):
    rows, width = x.shape
    got = exchange(x, axis, groups).reshape(parts, rows // parts, width)
    return jnp.sum(got.astype(jnp.float32), axis=0)


def split_high(x):
    high = lax.reduce_precision(x, 8, 7)
    return high, x - high


def ctx_shift(x, shift):
    return lax.ppermute(x, "ctx", [(i, (i + 2 * shift) % 8) for i in range(8)])


def ctx_swap(x):
    return lax.ppermute(x, "ctx", [(i, i ^ 1) for i in range(8)])


def rows_at(x, index, count):
    return lax.dynamic_slice_in_dim(x, index * count, count, axis=0)


def ctx_scatter(x):
    core = lax.axis_index("ctx") % 2
    chip = lax.axis_index("ctx") // 2
    half_rows = x.shape[0] // 2
    own_rows = half_rows // 4
    x = x.astype(jnp.float16)
    other = ctx_swap(rows_at(x, 1 - core, half_rows))
    pair = (
        rows_at(x, core, half_rows).astype(jnp.float32) + other.astype(jnp.float32)
    ).astype(jnp.float16)
    got = [ctx_shift(rows_at(pair, (chip + shift) % 4, own_rows), shift) for shift in (1, 3, 2)]
    own = rows_at(pair, chip, own_rows).astype(jnp.float32)
    for piece in got:
        own = own + piece.astype(jnp.float32)
    return own


def ctx_gather(own):
    core = lax.axis_index("ctx") % 2
    chip = lax.axis_index("ctx") // 2
    own_rows, width = own.shape
    from_one, from_three, from_two = [ctx_shift(own, shift) for shift in (1, 3, 2)]
    half = jnp.zeros((4 * own_rows, width), own.dtype)
    for piece, shift in ((own, 0), (from_one, 1), (from_three, 3), (from_two, 2)):
        half = lax.dynamic_update_slice_in_dim(half, piece, (chip + 4 - shift) % 4 * own_rows, axis=0)
    other = ctx_swap(half)
    first = jnp.where(core == 0, half, other)
    second = jnp.where(core == 0, other, half)
    return jnp.concatenate([first, second], axis=0)


def y_shift(x, shift):
    return lax.ppermute(
        x, "exp", [(i, (i + NZ * shift) % (NY * NZ)) for i in range(NY * NZ)]
    )


def ring_sum_over_y(block, far):
    y = lax.axis_index("exp") // NZ
    split = 512
    from_down = y_shift(far[:, :split], 1)
    from_up = y_shift(far[:, split:], 3)
    up = block((y + 1) % NY)
    up_late = y_shift(up[:, split:], 1)
    down = block((y + 3) % NY)
    down_late = y_shift(down[:, :split], 3)
    up_sum = (up[:, :split].astype(jnp.float32) + from_down.astype(jnp.float32)).astype(up.dtype)
    up_sum = y_shift(up_sum, 1)
    down_sum = (down[:, split:].astype(jnp.float32) + from_up.astype(jnp.float32)).astype(up.dtype)
    down_sum = y_shift(down_sum, 3)
    own = block(y).astype(jnp.float32)
    left = own[:, :split] + up_sum.astype(jnp.float32) + down_late.astype(jnp.float32)
    right = own[:, split:] + up_late.astype(jnp.float32) + down_sum.astype(jnp.float32)
    return jnp.concatenate([left, right], axis=1).astype(up.dtype)


def unit_backward(gate_sum, up_sum, back_sum, slot_prob):
    gate_sigmoid = jax.nn.sigmoid(gate_sum)
    gate_silu = gate_sum * gate_sigmoid
    prob_part = jnp.sum(gate_silu * up_sum * back_sum, axis=1)
    scaled_back = slot_prob[:, None] * back_sum
    gate_grad = (
        scaled_back * up_sum * gate_sigmoid * (1.0 + gate_sum * (1.0 - gate_sigmoid))
    ).astype(jnp.bfloat16)
    up_grad = (scaled_back * gate_silu).astype(jnp.bfloat16)
    return (gate_grad, up_grad, prob_part)


def local(
    logits,
    head_weight,
    token_ids,
    slab_order,
    token_weights,
    moe_input,
    routes,
    probs,
    w_gate,
    w_up,
    w_down,
):
    ctx_count = lax.axis_size("ctx")
    exp_count = lax.axis_size("exp")
    row_count, vocab_width = logits.shape
    seq_length = row_count * ctx_count
    all_logits = lax.all_gather(logits, "ctx", axis=0, tiled=True)

    token_count, route_count = routes.shape
    feature_width = moe_input.shape[1]
    capacity = min(token_count, 2 * token_count * route_count // exp_count)
    slot_count = exp_count * capacity
    route_list = routes.reshape(-1)
    expert_match = (route_list[:, None] == jnp.arange(exp_count, dtype=jnp.int32)[None, :]).astype(
        jnp.int32
    )
    route_rank = jnp.sum((jnp.cumsum(expert_match, axis=0) - 1) * expert_match, axis=1)
    slot_of_route = route_list * capacity + route_rank
    chosen = (jnp.arange(slot_count, dtype=jnp.int32)[:, None] == slot_of_route[None, :]).astype(
        jnp.float32
    )
    slot_owner = jnp.sum(chosen.reshape(slot_count, token_count, route_count), axis=2).astype(
        jnp.bfloat16
    )

    scores = logits.astype(jnp.float32)
    local_max = jnp.max(scores, axis=1)
    local_sum = jnp.sum(jnp.exp(scores - local_max[:, None]), axis=1)
    send_prob = jnp.dot(
        chosen, probs.reshape(-1).astype(jnp.float32), precision=lax.Precision.HIGHEST
    ).reshape(exp_count, capacity)
    send_input = jnp.dot(slot_owner, moe_input, preferred_element_type=jnp.float32).astype(
        jnp.bfloat16
    )
    packed = jnp.concatenate(
        [
            jnp.broadcast_to(local_max[None], (exp_count, row_count)),
            jnp.broadcast_to(local_sum[None], (exp_count, row_count)),
            jnp.pad(send_prob, ((0, 0), (0, 128 - capacity))),
        ],
        axis=1,
    )
    packed = exchange(packed, "exp")
    all_max = packed[:, :row_count]
    row_max = jnp.max(all_max, axis=0)
    row_total = jnp.sum(packed[:, row_count : 2 * row_count] * jnp.exp(all_max - row_max), axis=0)
    flat_prob = packed[:, 2 * row_count : 2 * row_count + capacity].reshape(-1)
    rows = jnp.concatenate([row_max, row_total, token_weights, token_ids.astype(jnp.float32)])
    rows = exchange(jnp.broadcast_to(rows[None], (ctx_count, 4 * row_count)), "ctx")
    rows = rows.reshape(ctx_count, 4, row_count).transpose(1, 0, 2).reshape(4, seq_length)
    rows, all_logits = lax.optimization_barrier((rows, all_logits))

    both_w = jnp.concatenate([w_gate[0], w_up[0]], axis=1)
    down_w = w_down[0]
    row_max, row_total, weights = rows[0], rows[1], rows[2]
    all_ids = rows[3].astype(jnp.int32)

    slab_count = slab_order.shape[0]
    next_ids = jnp.concatenate([all_ids[1:], all_ids[-1:]]).reshape(slab_count, SLAB)
    slab_match = slab_order[:, None] == jnp.arange(slab_count, dtype=jnp.int32)[None, :]
    target = jnp.sum(jnp.where(slab_match[:, :, None], next_ids[None], 0), axis=1).reshape(-1)
    position = (slab_order[:, None] * SLAB + jnp.arange(SLAB, dtype=jnp.int32)).reshape(-1)
    has_target = position < seq_length - 1
    local_target = target - lax.axis_index("exp") * vocab_width
    weighting = jnp.where(has_target, weights, 0.0)
    columns = jnp.arange(vocab_width, dtype=jnp.int32)[None, :]
    per_row = jnp.stack([row_max, row_total, weighting, local_target.astype(jnp.float32)])

    def upstream_block(q):
        count = seq_length // NY
        top, total, weight, aim = lax.dynamic_slice_in_dim(per_row, q * count, count, axis=1)
        is_target = columns == aim.astype(jnp.int32)[:, None]
        logit_grads = (
            weight[:, None]
            * (
                jnp.exp(rows_at(all_logits, q, count).astype(jnp.float32) - top[:, None])
                / total[:, None]
                - is_target.astype(jnp.float32)
            )
        ).astype(jnp.bfloat16)
        partial = jnp.dot(logit_grads, head_weight, preferred_element_type=jnp.float32)
        return (partial * 4096.0).astype(jnp.float16)

    far = upstream_block((lax.axis_index("exp") // NZ + 2) % NY)
    far, send_input = lax.optimization_barrier((far, send_input))
    flat_inputs = exchange(send_input, "exp")
    over_y = ring_sum_over_y(upstream_block, far)
    part_both = jnp.dot(flat_inputs, both_w, preferred_element_type=jnp.float32)
    over_y, part_both = lax.optimization_barrier((over_y, part_both.astype(jnp.float16)))
    upstream = exchange_sum(over_y, "exp", Z_GROUPS, NZ) * (1.0 / 4096.0)
    upstream_sent = upstream.astype(jnp.bfloat16)

    send_upstream = jnp.dot(slot_owner, upstream_sent, preferred_element_type=jnp.float32)
    flat_upstream = exchange(send_upstream.astype(jnp.bfloat16), "exp")
    both_sum = ctx_scatter(part_both)
    flat_upstream, both_sum = lax.optimization_barrier((flat_upstream, both_sum))
    part_back = lax.dot_general(
        flat_upstream, down_w, CONTRACT_LAST, preferred_element_type=jnp.float32
    )
    back_sum = ctx_scatter(part_back)

    hidden = w_gate.shape[2]
    own_count = slot_count // ctx_count
    ctx_index = lax.axis_index("ctx")
    own_prob = rows_at(flat_prob, ctx_index % 2 * 4 + ctx_index // 2, own_count)
    gate_grad, up_grad, prob_grad = unit_backward(
        both_sum[:, :hidden], both_sum[:, hidden:], back_sum, own_prob
    )
    prob_high, prob_low = split_high(prob_grad)
    lane = jnp.arange(128, dtype=jnp.int32)[None, :]
    prob_block = jnp.where(
        lane == 0, prob_high[:, None], jnp.where(lane == 1, prob_low[:, None], 0)
    ).astype(jnp.bfloat16)
    grads = ctx_gather(jnp.concatenate([gate_grad, up_grad, prob_block], axis=1))
    input_grad = lax.dot_general(
        grads[:, : 2 * hidden], both_w, CONTRACT_LAST, preferred_element_type=jnp.float32
    )
    back = exchange(
        jnp.concatenate([input_grad.astype(jnp.bfloat16), grads[:, 2 * hidden :]], axis=1), "exp"
    )
    d_x = upstream + lax.dot_general(
        slot_owner,
        back[:, :feature_width],
        (((0,), (0,)), ((), ())),
        preferred_element_type=jnp.float32,
    )
    back_prob = back[:, feature_width].astype(jnp.float32) + back[:, feature_width + 1].astype(
        jnp.float32
    )
    d_prob = jnp.dot(back_prob, chosen, precision=lax.Precision.HIGHEST).reshape(
        token_count, route_count
    )
    return (d_x, d_prob)


def solution(mesh):
    placed = (
        P("ctx", "exp"),
        P("exp", "ctx"),
        P("ctx"),
        P(),
        P("ctx"),
        P("exp", "ctx"),
        P("exp", None),
        P("exp", None),
        P("exp", "ctx", None),
        P("exp", "ctx", None),
        P("exp", None, "ctx"),
    )
    return jax.shard_map(
        local,
        mesh=mesh,
        in_specs=placed,
        out_specs=(P("exp", "ctx"), P("exp", None)),
        check_vma=False,
    )
```

```python
import jax
import jax.numpy as jnp
from jax import lax
from jax.sharding import PartitionSpec as P

SLAB = 64
NY, NZ = 4, 8
Z_GROUPS = [[y * NZ + z for z in range(NZ)] for y in range(NY)]
CONTRACT_LAST = (((1,), (1,)), ((), ()))


def exchange(x, axis, groups=None):
    return lax.all_to_all(x, axis, 0, 0, tiled=True, axis_index_groups=groups)


def exchange_sum(x, axis, groups, parts):
    rows, width = x.shape
    got = exchange(x, axis, groups).reshape(parts, rows // parts, width)
    return jnp.sum(got.astype(jnp.float32), axis=0)


def split_high(x):
    high = lax.reduce_precision(x, 8, 7)
    return high, x - high


def ctx_shift(x, shift):
    return lax.ppermute(x, "ctx", [(i, (i + 2 * shift) % 8) for i in range(8)])


def ctx_swap(x):
    return lax.ppermute(x, "ctx", [(i, i ^ 1) for i in range(8)])


def rows_at(x, index, count):
    return lax.dynamic_slice_in_dim(x, index * count, count, axis=0)


def ctx_scatter(x):
    core = lax.axis_index("ctx") % 2
    chip = lax.axis_index("ctx") // 2
    half_rows = x.shape[0] // 2
    own_rows = half_rows // 4
    x = x.astype(jnp.float16)
    other = ctx_swap(rows_at(x, 1 - core, half_rows))
    pair = (
        rows_at(x, core, half_rows).astype(jnp.float32) + other.astype(jnp.float32)
    ).astype(jnp.float16)
    got = [ctx_shift(rows_at(pair, (chip + shift) % 4, own_rows), shift) for shift in (1, 3, 2)]
    own = rows_at(pair, chip, own_rows).astype(jnp.float32)
    for piece in got:
        own = own + piece.astype(jnp.float32)
    return own


def ctx_gather(own):
    core = lax.axis_index("ctx") % 2
    chip = lax.axis_index("ctx") // 2
    own_rows, width = own.shape
    from_one, from_three, from_two = [ctx_shift(own, shift) for shift in (1, 3, 2)]
    half = jnp.zeros((4 * own_rows, width), own.dtype)
    for piece, shift in ((own, 0), (from_one, 1), (from_three, 3), (from_two, 2)):
        half = lax.dynamic_update_slice_in_dim(half, piece, (chip + 4 - shift) % 4 * own_rows, axis=0)
    other = ctx_swap(half)
    first = jnp.where(core == 0, half, other)
    second = jnp.where(core == 0, other, half)
    return jnp.concatenate([first, second], axis=0)


def y_shift(x, shift):
    return lax.ppermute(
        x, "exp", [(i, (i + NZ * shift) % (NY * NZ)) for i in range(NY * NZ)]
    )


def ring_sum_over_y(block, far, per_row):
    y = lax.axis_index("exp") // NZ
    split = far.shape[0] // 2
    from_down = y_shift(far[:split], 1)
    from_up = y_shift(far[split:], 3)
    from_down, from_up, per_row = lax.optimization_barrier((from_down, from_up, per_row))
    up = block((y + 1) % NY, per_row)
    up_late = y_shift(up[split:], 1)
    down = block((y + 3) % NY, per_row)
    down_late = y_shift(down[:split], 3)
    up_sum = (up[:split].astype(jnp.float32) + from_down.astype(jnp.float32)).astype(up.dtype)
    up_sum = y_shift(up_sum, 1)
    down_sum = (down[split:].astype(jnp.float32) + from_up.astype(jnp.float32)).astype(up.dtype)
    down_sum = y_shift(down_sum, 3)
    own = block(y, per_row).astype(jnp.float32)
    first = own[:split] + up_sum.astype(jnp.float32) + down_late.astype(jnp.float32)
    second = own[split:] + up_late.astype(jnp.float32) + down_sum.astype(jnp.float32)
    return jnp.concatenate([first, second], axis=0).astype(up.dtype)


def unit_backward(gate_sum, up_sum, back_sum, slot_prob):
    gate_sigmoid = jax.nn.sigmoid(gate_sum)
    gate_silu = gate_sum * gate_sigmoid
    prob_part = jnp.sum(gate_silu * up_sum * back_sum, axis=1)
    scaled_back = slot_prob[:, None] * back_sum
    gate_grad = (
        scaled_back * up_sum * gate_sigmoid * (1.0 + gate_sum * (1.0 - gate_sigmoid))
    ).astype(jnp.bfloat16)
    up_grad = (scaled_back * gate_silu).astype(jnp.bfloat16)
    return (gate_grad, up_grad, prob_part)


def local(
    logits,
    head_weight,
    token_ids,
    slab_order,
    token_weights,
    moe_input,
    routes,
    probs,
    w_gate,
    w_up,
    w_down,
):
    ctx_count = lax.axis_size("ctx")
    exp_count = lax.axis_size("exp")
    row_count, vocab_width = logits.shape
    seq_length = row_count * ctx_count
    all_logits = lax.all_gather(logits, "ctx", axis=0, tiled=True)

    token_count, route_count = routes.shape
    feature_width = moe_input.shape[1]
    capacity = min(token_count, 2 * token_count * route_count // exp_count)
    slot_count = exp_count * capacity
    route_list = routes.reshape(-1)
    expert_match = (route_list[:, None] == jnp.arange(exp_count, dtype=jnp.int32)[None, :]).astype(
        jnp.int32
    )
    route_rank = jnp.sum((jnp.cumsum(expert_match, axis=0) - 1) * expert_match, axis=1)
    slot_of_route = route_list * capacity + route_rank
    chosen = (jnp.arange(slot_count, dtype=jnp.int32)[:, None] == slot_of_route[None, :]).astype(
        jnp.float32
    )
    slot_owner = jnp.sum(chosen.reshape(slot_count, token_count, route_count), axis=2).astype(
        jnp.bfloat16
    )

    scores = logits.astype(jnp.float32)
    local_max = jnp.max(scores, axis=1)
    local_sum = jnp.sum(jnp.exp(scores - local_max[:, None]), axis=1)
    send_prob = jnp.dot(
        chosen, probs.reshape(-1).astype(jnp.float32), precision=lax.Precision.HIGHEST
    ).reshape(exp_count, capacity)
    send_input = jnp.dot(slot_owner, moe_input, preferred_element_type=jnp.float32).astype(
        jnp.bfloat16
    )
    packed = jnp.concatenate(
        [
            jnp.broadcast_to(local_max[None], (exp_count, row_count)),
            jnp.broadcast_to(local_sum[None], (exp_count, row_count)),
            jnp.pad(send_prob, ((0, 0), (0, 128 - capacity))),
        ],
        axis=1,
    )
    packed = exchange(packed, "exp")
    all_max = packed[:, :row_count]
    row_max = jnp.max(all_max, axis=0)
    row_total = jnp.sum(packed[:, row_count : 2 * row_count] * jnp.exp(all_max - row_max), axis=0)
    flat_prob = packed[:, 2 * row_count : 2 * row_count + capacity].reshape(-1)
    rows = jnp.concatenate([row_max, row_total, token_weights, token_ids.astype(jnp.float32)])
    rows = exchange(jnp.broadcast_to(rows[None], (ctx_count, 4 * row_count)), "ctx")
    rows = rows.reshape(ctx_count, 4, row_count).transpose(1, 0, 2).reshape(4, seq_length)
    rows, all_logits = lax.optimization_barrier((rows, all_logits))

    gate_w = w_gate[0]
    up_w = w_up[0]
    down_w = w_down[0]
    row_max, row_total, weights = rows[0], rows[1], rows[2]
    all_ids = rows[3].astype(jnp.int32)

    slab_count = slab_order.shape[0]
    next_ids = jnp.concatenate([all_ids[1:], all_ids[-1:]]).reshape(slab_count, SLAB)
    slab_match = slab_order[:, None] == jnp.arange(slab_count, dtype=jnp.int32)[None, :]
    target = jnp.sum(jnp.where(slab_match[:, :, None], next_ids[None], 0), axis=1).reshape(-1)
    position = (slab_order[:, None] * SLAB + jnp.arange(SLAB, dtype=jnp.int32)).reshape(-1)
    has_target = position < seq_length - 1
    local_target = target - lax.axis_index("exp") * vocab_width
    weighting = jnp.where(has_target, weights, 0.0)
    columns = jnp.arange(vocab_width, dtype=jnp.int32)[None, :]
    per_row = jnp.stack([row_max, row_total, weighting, local_target.astype(jnp.float32)])

    def upstream_block(q, per_row):
        count = seq_length // NY
        top, total, weight, aim = lax.dynamic_slice_in_dim(per_row, q * count, count, axis=1)
        is_target = columns == aim.astype(jnp.int32)[:, None]
        logit_grads = (
            weight[:, None]
            * (
                jnp.exp(rows_at(all_logits, q, count).astype(jnp.float32) - top[:, None])
                / total[:, None]
                - is_target.astype(jnp.float32)
            )
        ).astype(jnp.bfloat16)
        partial = jnp.dot(logit_grads, head_weight, preferred_element_type=jnp.float32)
        return (partial * 4096.0).astype(jnp.float16)

    far = upstream_block((lax.axis_index("exp") // NZ + 2) % NY, per_row)
    far, send_input = lax.optimization_barrier((far, send_input))
    flat_inputs = exchange(send_input, "exp")
    over_y = ring_sum_over_y(upstream_block, far, per_row)
    flat_inputs, over_y = lax.optimization_barrier((flat_inputs, over_y))
    part_both = jnp.concatenate(
        [
            jnp.dot(flat_inputs, weight, preferred_element_type=jnp.float32).astype(jnp.float16)
            for weight in (gate_w, up_w)
        ],
        axis=1,
    )
    upstream = exchange_sum(over_y, "exp", Z_GROUPS, NZ) * (1.0 / 4096.0)
    upstream_sent = upstream.astype(jnp.bfloat16)

    send_upstream = jnp.dot(slot_owner, upstream_sent, preferred_element_type=jnp.float32).astype(
        jnp.bfloat16
    )
    send_upstream, part_both = lax.optimization_barrier((send_upstream, part_both))
    flat_upstream = exchange(send_upstream, "exp")
    both_sum = ctx_scatter(part_both)
    flat_upstream, both_sum = lax.optimization_barrier((flat_upstream, both_sum))
    part_back = lax.dot_general(
        flat_upstream, down_w, CONTRACT_LAST, preferred_element_type=jnp.float32
    )
    back_sum = ctx_scatter(part_back)

    hidden = w_gate.shape[2]
    own_count = slot_count // ctx_count
    ctx_index = lax.axis_index("ctx")
    own_prob = rows_at(flat_prob, ctx_index % 2 * 4 + ctx_index // 2, own_count)
    gate_grad, up_grad, prob_grad = unit_backward(
        both_sum[:, :hidden], both_sum[:, hidden:], back_sum, own_prob
    )
    prob_high, prob_low = split_high(prob_grad)
    lane = jnp.arange(128, dtype=jnp.int32)[None, :]
    prob_block = jnp.where(
        lane == 0, prob_high[:, None], jnp.where(lane == 1, prob_low[:, None], 0)
    ).astype(jnp.bfloat16)
    grads = ctx_gather(jnp.concatenate([gate_grad, up_grad, prob_block], axis=1))
    input_grad = lax.dot_general(
        grads[:, :hidden], gate_w, CONTRACT_LAST, preferred_element_type=jnp.float32
    ) + lax.dot_general(
        grads[:, hidden : 2 * hidden], up_w, CONTRACT_LAST, preferred_element_type=jnp.float32
    )
    back = exchange(
        jnp.concatenate([input_grad.astype(jnp.bfloat16), grads[:, 2 * hidden :]], axis=1), "exp"
    )
    d_x = upstream + lax.dot_general(
        slot_owner,
        back[:, :feature_width],
        (((0,), (0,)), ((), ())),
        preferred_element_type=jnp.float32,
    )
    d_prob = jnp.sum(
        lax.dot_general(
            back[:, feature_width : feature_width + 2],
            chosen.astype(jnp.bfloat16),
            (((0,), (0,)), ((), ())),
            preferred_element_type=jnp.float32,
        ),
        axis=0,
    ).reshape(token_count, route_count)
    return (d_x, d_prob)


def solution(mesh):
    placed = (
        P("ctx", "exp"),
        P("exp", "ctx"),
        P("ctx"),
        P(),
        P("ctx"),
        P("exp", "ctx"),
        P("exp", None),
        P("exp", None),
        P("exp", "ctx", None),
        P("exp", "ctx", None),
        P("exp", None, "ctx"),
    )
    return jax.shard_map(
        local,
        mesh=mesh,
        in_specs=placed,
        out_specs=(P("exp", "ctx"), P("exp", None)),
        check_vma=False,
    )
```

```python
import jax
import jax.numpy as jnp
from jax import lax
from jax.sharding import PartitionSpec as P

SLAB = 64
NY, NZ = 4, 8
Z_GROUPS = [[y * NZ + z for z in range(NZ)] for y in range(NY)]
CONTRACT_LAST = (((1,), (1,)), ((), ()))


def exchange(x, axis, groups=None):
    return lax.all_to_all(x, axis, 0, 0, tiled=True, axis_index_groups=groups)


def exchange_sum(x, axis, groups, parts):
    rows, width = x.shape
    got = exchange(x, axis, groups).reshape(parts, rows // parts, width)
    return jnp.sum(got.astype(jnp.float32), axis=0)


def split_high(x):
    high = lax.reduce_precision(x, 8, 7)
    return high, x - high


def ctx_shift(x, shift):
    return lax.ppermute(x, "ctx", [(i, (i + 2 * shift) % 8) for i in range(8)])


def ctx_swap(x):
    return lax.ppermute(x, "ctx", [(i, i ^ 1) for i in range(8)])


def rows_at(x, index, count):
    return lax.dynamic_slice_in_dim(x, index * count, count, axis=0)


def ctx_scatter(x):
    core = lax.axis_index("ctx") % 2
    chip = lax.axis_index("ctx") // 2
    half_rows = x.shape[0] // 2
    own_rows = half_rows // 4
    x = x.astype(jnp.float16)
    other = ctx_swap(rows_at(x, 1 - core, half_rows))
    pair = (
        rows_at(x, core, half_rows).astype(jnp.float32) + other.astype(jnp.float32)
    ).astype(jnp.float16)
    got = [ctx_shift(rows_at(pair, (chip + shift) % 4, own_rows), shift) for shift in (1, 3, 2)]
    own = rows_at(pair, chip, own_rows).astype(jnp.float32)
    for piece in got:
        own = own + piece.astype(jnp.float32)
    return own


def ctx_gather(own):
    core = lax.axis_index("ctx") % 2
    chip = lax.axis_index("ctx") // 2
    own_rows, width = own.shape
    from_one, from_three, from_two = [ctx_shift(own, shift) for shift in (1, 3, 2)]
    half = jnp.zeros((4 * own_rows, width), own.dtype)
    for piece, shift in ((own, 0), (from_one, 1), (from_three, 3), (from_two, 2)):
        half = lax.dynamic_update_slice_in_dim(half, piece, (chip + 4 - shift) % 4 * own_rows, axis=0)
    other = ctx_swap(half)
    first = jnp.where(core == 0, half, other)
    second = jnp.where(core == 0, other, half)
    return jnp.concatenate([first, second], axis=0)


def y_shift(x, shift):
    return lax.ppermute(
        x, "exp", [(i, (i + NZ * shift) % (NY * NZ)) for i in range(NY * NZ)]
    )


def ring_sum_over_y(block, far, per_row):
    y = lax.axis_index("exp") // NZ
    split = far.shape[0] // 2
    from_down = y_shift(far[:split], 1)
    from_up = y_shift(far[split:], 3)
    up = block((y + 1) % NY, per_row)
    up_late = y_shift(up[split:], 1)
    down = block((y + 3) % NY, per_row)
    down_late = y_shift(down[:split], 3)
    up_sum = (up[:split].astype(jnp.float32) + from_down.astype(jnp.float32)).astype(up.dtype)
    up_sum = y_shift(up_sum, 1)
    down_sum = (down[split:].astype(jnp.float32) + from_up.astype(jnp.float32)).astype(up.dtype)
    down_sum = y_shift(down_sum, 3)
    own = block(y, per_row).astype(jnp.float32)
    first = own[:split] + up_sum.astype(jnp.float32) + down_late.astype(jnp.float32)
    second = own[split:] + up_late.astype(jnp.float32) + down_sum.astype(jnp.float32)
    return jnp.concatenate([first, second], axis=0).astype(up.dtype)


def unit_backward(gate_sum, up_sum, back_sum, slot_prob):
    gate_sigmoid = jax.nn.sigmoid(gate_sum)
    gate_silu = gate_sum * gate_sigmoid
    prob_part = jnp.sum(gate_silu * up_sum * back_sum, axis=1)
    scaled_back = slot_prob[:, None] * back_sum
    gate_grad = (
        scaled_back * up_sum * gate_sigmoid * (1.0 + gate_sum * (1.0 - gate_sigmoid))
    ).astype(jnp.bfloat16)
    up_grad = (scaled_back * gate_silu).astype(jnp.bfloat16)
    return (gate_grad, up_grad, prob_part)


def local(
    logits,
    head_weight,
    token_ids,
    slab_order,
    token_weights,
    moe_input,
    routes,
    probs,
    w_gate,
    w_up,
    w_down,
):
    ctx_count = lax.axis_size("ctx")
    exp_count = lax.axis_size("exp")
    row_count, vocab_width = logits.shape
    seq_length = row_count * ctx_count
    all_logits = lax.all_gather(logits, "ctx", axis=0, tiled=True)

    token_count, route_count = routes.shape
    feature_width = moe_input.shape[1]
    capacity = min(token_count, 2 * token_count * route_count // exp_count)
    slot_count = exp_count * capacity
    route_list = routes.reshape(-1)
    expert_match = (route_list[:, None] == jnp.arange(exp_count, dtype=jnp.int32)[None, :]).astype(
        jnp.int32
    )
    route_rank = jnp.sum((jnp.cumsum(expert_match, axis=0) - 1) * expert_match, axis=1)
    slot_of_route = route_list * capacity + route_rank
    chosen = (jnp.arange(slot_count, dtype=jnp.int32)[:, None] == slot_of_route[None, :]).astype(
        jnp.float32
    )
    slot_owner = jnp.sum(chosen.reshape(slot_count, token_count, route_count), axis=2).astype(
        jnp.bfloat16
    )

    scores = logits.astype(jnp.float32)
    local_max = jnp.max(scores, axis=1)
    local_sum = jnp.sum(jnp.exp(scores - local_max[:, None]), axis=1)
    send_prob = jnp.dot(
        chosen.astype(jnp.bfloat16), probs.reshape(-1), preferred_element_type=jnp.float32
    ).astype(jnp.bfloat16)
    send_input = jnp.dot(slot_owner, moe_input, preferred_element_type=jnp.float32).astype(
        jnp.bfloat16
    )
    sum_high, sum_rest = split_high(local_sum)
    sum_mid, sum_low = split_high(sum_rest)
    stats = jnp.stack([local_max, sum_high, sum_mid, sum_low]).astype(jnp.bfloat16)
    extra = jnp.concatenate(
        [
            jnp.broadcast_to(stats[None], (exp_count, 4, row_count)),
            jnp.pad(
                send_prob.reshape(exp_count, 1, capacity),
                ((0, 0), (0, capacity - 5), (0, row_count - capacity)),
            ),
        ],
        axis=1,
    ).reshape(slot_count, row_count)
    got = exchange(jnp.concatenate([send_input, extra], axis=1), "exp")
    flat_inputs = got[:, :feature_width]
    extra = got[:, feature_width:].reshape(exp_count, capacity, row_count)
    flat_prob = extra[:, 4, :capacity].reshape(-1).astype(jnp.float32)
    stats = extra[:, :4].astype(jnp.float32)
    all_max = stats[:, 0]
    row_max = jnp.max(all_max, axis=0)
    row_total = jnp.sum(
        (stats[:, 1] + stats[:, 2] + stats[:, 3]) * jnp.exp(all_max - row_max), axis=0
    )
    rows = jnp.concatenate([row_max, row_total, token_weights, token_ids.astype(jnp.float32)])
    rows = exchange(jnp.broadcast_to(rows[None], (ctx_count, 4 * row_count)), "ctx")
    rows = rows.reshape(ctx_count, 4, row_count).transpose(1, 0, 2).reshape(4, seq_length)
    rows, all_logits = lax.optimization_barrier((rows, all_logits))

    gate_w = w_gate[0]
    up_w = w_up[0]
    down_w = w_down[0]
    row_max, row_total, weights = rows[0], rows[1], rows[2]
    all_ids = rows[3].astype(jnp.int32)

    one = 1 - jnp.minimum(lax.axis_index("ctx"), 0)
    head_weight = lax.optimization_barrier(head_weight * one.astype(jnp.bfloat16))

    slab_count = slab_order.shape[0]
    next_ids = jnp.concatenate([all_ids[1:], all_ids[-1:]]).reshape(slab_count, SLAB)
    slab_match = slab_order[:, None] == jnp.arange(slab_count, dtype=jnp.int32)[None, :]
    target = jnp.sum(jnp.where(slab_match[:, :, None], next_ids[None], 0), axis=1).reshape(-1)
    position = (slab_order[:, None] * SLAB + jnp.arange(SLAB, dtype=jnp.int32)).reshape(-1)
    has_target = position < seq_length - 1
    local_target = target - lax.axis_index("exp") * vocab_width
    weighting = jnp.where(has_target, weights, 0.0)
    columns = jnp.arange(vocab_width, dtype=jnp.int32)[None, :]
    per_row = jnp.stack([row_max, row_total, weighting, local_target.astype(jnp.float32)])

    def upstream_block(q, per_row):
        count = seq_length // NY
        top, total, weight, aim = lax.dynamic_slice_in_dim(per_row, q * count, count, axis=1)
        is_target = columns == aim.astype(jnp.int32)[:, None]
        logit_grads = (
            weight[:, None]
            * (
                jnp.exp(rows_at(all_logits, q, count).astype(jnp.float32) - top[:, None])
                / total[:, None]
                - is_target.astype(jnp.float32)
            )
        ).astype(jnp.bfloat16)
        partial = jnp.dot(logit_grads, head_weight, preferred_element_type=jnp.float32)
        return (partial * 4096.0).astype(jnp.float16)

    far = upstream_block((lax.axis_index("exp") // NZ + 2) % NY, per_row)
    far, flat_inputs = lax.optimization_barrier((far, flat_inputs))
    over_y = ring_sum_over_y(upstream_block, far, per_row)
    part_both = jnp.concatenate(
        [
            jnp.dot(flat_inputs, weight, preferred_element_type=jnp.float32).astype(jnp.float16)
            for weight in (gate_w, up_w)
        ],
        axis=1,
    )
    both_sum = ctx_scatter(part_both)
    upstream = exchange_sum(over_y, "exp", Z_GROUPS, NZ) * (1.0 / 4096.0)
    upstream_sent = upstream.astype(jnp.bfloat16)

    send_upstream = jnp.dot(slot_owner, upstream_sent, preferred_element_type=jnp.float32).astype(
        jnp.bfloat16
    )
    flat_upstream = exchange(send_upstream, "exp")
    flat_upstream, both_sum = lax.optimization_barrier((flat_upstream, both_sum))
    part_back = lax.dot_general(
        flat_upstream, down_w, CONTRACT_LAST, preferred_element_type=jnp.float32
    )
    back_sum = ctx_scatter(part_back)

    hidden = w_gate.shape[2]
    own_count = slot_count // ctx_count
    ctx_index = lax.axis_index("ctx")
    own_prob = rows_at(flat_prob, ctx_index % 2 * 4 + ctx_index // 2, own_count)
    gate_grad, up_grad, prob_grad = unit_backward(
        both_sum[:, :hidden], both_sum[:, hidden:], back_sum, own_prob
    )
    prob_high, prob_low = split_high(prob_grad)
    lane = jnp.arange(128, dtype=jnp.int32)[None, :]
    prob_block = jnp.where(
        lane == 0, prob_high[:, None], jnp.where(lane == 1, prob_low[:, None], 0)
    ).astype(jnp.bfloat16)
    grads = ctx_gather(jnp.concatenate([gate_grad, up_grad, prob_block], axis=1))
    input_grad = lax.dot_general(
        grads[:, :hidden], gate_w, CONTRACT_LAST, preferred_element_type=jnp.float32
    ) + lax.dot_general(
        grads[:, hidden : 2 * hidden], up_w, CONTRACT_LAST, preferred_element_type=jnp.float32
    )
    back = exchange(
        jnp.concatenate([input_grad.astype(jnp.bfloat16), grads[:, 2 * hidden :]], axis=1), "exp"
    )
    d_x = upstream + lax.dot_general(
        slot_owner,
        back[:, :feature_width],
        (((0,), (0,)), ((), ())),
        preferred_element_type=jnp.float32,
    )
    d_prob = jnp.sum(
        lax.dot_general(
            back[:, feature_width : feature_width + 2],
            chosen.astype(jnp.bfloat16),
            (((0,), (0,)), ((), ())),
            preferred_element_type=jnp.float32,
        ),
        axis=0,
    ).reshape(token_count, route_count)
    return (d_x, d_prob)


def solution(mesh):
    placed = (
        P("ctx", "exp"),
        P("exp", "ctx"),
        P("ctx"),
        P(),
        P("ctx"),
        P("exp", "ctx"),
        P("exp", None),
        P("exp", None),
        P("exp", "ctx", None),
        P("exp", "ctx", None),
        P("exp", None, "ctx"),
    )
    return jax.shard_map(
        local,
        mesh=mesh,
        in_specs=placed,
        out_specs=(P("exp", "ctx"), P("exp", None)),
        check_vma=False,
    )
```

```python
import jax
import jax.numpy as jnp
from jax import lax
from jax.sharding import PartitionSpec as P

SLAB = 64
NY, NZ = 4, 8
Z_GROUPS = [[y * NZ + z for z in range(NZ)] for y in range(NY)]
CONTRACT_LAST = (((1,), (1,)), ((), ()))


def exchange(x, axis, groups=None):
    return lax.all_to_all(x, axis, 0, 0, tiled=True, axis_index_groups=groups)


def exchange_sum(x, axis, groups, parts):
    rows, width = x.shape
    got = exchange(x, axis, groups).reshape(parts, rows // parts, width)
    return jnp.sum(got.astype(jnp.float32), axis=0)


def split_high(x):
    high = lax.reduce_precision(x, 8, 7)
    return high, x - high


def ctx_shift(x, shift):
    return lax.ppermute(x, "ctx", [(i, (i + 2 * shift) % 8) for i in range(8)])


def ctx_swap(x):
    return lax.ppermute(x, "ctx", [(i, i ^ 1) for i in range(8)])


def rows_at(x, index, count):
    return lax.dynamic_slice_in_dim(x, index * count, count, axis=0)


def ctx_scatter(x, after=None):
    core = lax.axis_index("ctx") % 2
    chip = lax.axis_index("ctx") // 2
    half_rows = x.shape[0] // 2
    own_rows = half_rows // 4
    x = x.astype(jnp.float16)
    other = ctx_swap(rows_at(x, 1 - core, half_rows))
    pair = (
        rows_at(x, core, half_rows).astype(jnp.float32) + other.astype(jnp.float32)
    ).astype(jnp.float16)
    if after is not None:
        pair, after = lax.optimization_barrier((pair, after))
    got = [ctx_shift(rows_at(pair, (chip + shift) % 4, own_rows), shift) for shift in (1, 3, 2)]
    own = rows_at(pair, chip, own_rows).astype(jnp.float32)
    for piece in got:
        own = own + piece.astype(jnp.float32)
    return own, after


def ctx_gather(own):
    core = lax.axis_index("ctx") % 2
    chip = lax.axis_index("ctx") // 2
    own_rows, width = own.shape
    from_one, from_three, from_two = [ctx_shift(own, shift) for shift in (1, 3, 2)]
    half = jnp.zeros((4 * own_rows, width), own.dtype)
    for piece, shift in ((own, 0), (from_one, 1), (from_three, 3), (from_two, 2)):
        half = lax.dynamic_update_slice_in_dim(half, piece, (chip + 4 - shift) % 4 * own_rows, axis=0)
    other = ctx_swap(half)
    first = jnp.where(core == 0, half, other)
    second = jnp.where(core == 0, other, half)
    return jnp.concatenate([first, second], axis=0)


def y_shift(x, shift):
    return lax.ppermute(
        x, "exp", [(i, (i + NZ * shift) % (NY * NZ)) for i in range(NY * NZ)]
    )


def ring_sum_over_y(block, far, per_row):
    y = lax.axis_index("exp") // NZ
    split = far.shape[0] // 2
    from_down = y_shift(far[:split], 1)
    from_up = y_shift(far[split:], 3)
    up = block((y + 1) % NY, per_row)
    up_late = y_shift(up[split:], 1)
    down = block((y + 3) % NY, per_row)
    down_late = y_shift(down[:split], 3)
    up_sum = (up[:split].astype(jnp.float32) + from_down.astype(jnp.float32)).astype(up.dtype)
    up_sum = y_shift(up_sum, 1)
    down_sum = (down[split:].astype(jnp.float32) + from_up.astype(jnp.float32)).astype(up.dtype)
    down_sum = y_shift(down_sum, 3)
    own = block(y, per_row).astype(jnp.float32)
    first = own[:split] + up_sum.astype(jnp.float32) + down_late.astype(jnp.float32)
    second = own[split:] + up_late.astype(jnp.float32) + down_sum.astype(jnp.float32)
    return jnp.concatenate([first, second], axis=0).astype(up.dtype)


def unit_backward(gate_sum, up_sum, back_sum, slot_prob):
    gate_sigmoid = jax.nn.sigmoid(gate_sum)
    gate_silu = gate_sum * gate_sigmoid
    prob_part = jnp.sum(gate_silu * up_sum * back_sum, axis=1)
    scaled_back = slot_prob[:, None] * back_sum
    gate_grad = (
        scaled_back * up_sum * gate_sigmoid * (1.0 + gate_sum * (1.0 - gate_sigmoid))
    ).astype(jnp.bfloat16)
    up_grad = (scaled_back * gate_silu).astype(jnp.bfloat16)
    return (gate_grad, up_grad, prob_part)


def local(
    logits,
    head_weight,
    token_ids,
    slab_order,
    token_weights,
    moe_input,
    routes,
    probs,
    w_gate,
    w_up,
    w_down,
):
    ctx_count = lax.axis_size("ctx")
    exp_count = lax.axis_size("exp")
    row_count, vocab_width = logits.shape
    seq_length = row_count * ctx_count
    all_logits = lax.all_gather(logits, "ctx", axis=0, tiled=True)

    token_count, route_count = routes.shape
    feature_width = moe_input.shape[1]
    capacity = min(token_count, 2 * token_count * route_count // exp_count)
    slot_count = exp_count * capacity
    route_list = routes.reshape(-1)
    expert_match = (route_list[:, None] == jnp.arange(exp_count, dtype=jnp.int32)[None, :]).astype(
        jnp.int32
    )
    route_rank = jnp.sum((jnp.cumsum(expert_match, axis=0) - 1) * expert_match, axis=1)
    slot_of_route = route_list * capacity + route_rank
    chosen = (jnp.arange(slot_count, dtype=jnp.int32)[:, None] == slot_of_route[None, :]).astype(
        jnp.float32
    )
    slot_owner = jnp.sum(chosen.reshape(slot_count, token_count, route_count), axis=2).astype(
        jnp.bfloat16
    )

    send_input = jnp.dot(slot_owner, moe_input, preferred_element_type=jnp.float32).astype(
        jnp.bfloat16
    )
    flat_inputs = exchange(send_input, "exp")

    scores = logits.astype(jnp.float32)
    local_max = jnp.max(scores, axis=1)
    local_sum = jnp.sum(jnp.exp(scores - local_max[:, None]), axis=1)
    own_rows = jnp.stack([local_max, local_sum, token_weights, token_ids.astype(jnp.float32)])
    rows = ctx_gather(jnp.pad(own_rows, ((0, 4), (0, 0))))
    rows = rows.reshape(2, 4, 8, row_count).transpose(2, 1, 0, 3).reshape(8, seq_length)
    weights = rows[2]
    all_ids = rows[3].astype(jnp.int32)
    send_prob = jnp.dot(
        chosen.astype(jnp.bfloat16), probs.reshape(-1), preferred_element_type=jnp.float32
    ).reshape(exp_count, capacity)
    packed = jnp.concatenate(
        [
            jnp.broadcast_to(rows[:2].reshape(1, -1), (exp_count, 2 * seq_length)),
            jnp.pad(send_prob, ((0, 0), (0, 128 - capacity))),
        ],
        axis=1,
    )
    packed, flat_inputs = lax.optimization_barrier((packed, flat_inputs))
    packed = exchange(packed, "exp")
    all_max = packed[:, :seq_length]
    row_max = jnp.max(all_max, axis=0)
    row_total = jnp.sum(packed[:, seq_length : 2 * seq_length] * jnp.exp(all_max - row_max), axis=0)
    flat_prob = packed[:, 2 * seq_length : 2 * seq_length + capacity].reshape(-1)

    gate_w = w_gate[0]
    up_w = w_up[0]
    down_w = w_down[0]
    one = 1 - jnp.minimum(lax.axis_index("ctx"), 0)
    head_weight = lax.optimization_barrier(head_weight * one.astype(jnp.bfloat16))

    slab_count = slab_order.shape[0]
    next_ids = jnp.concatenate([all_ids[1:], all_ids[-1:]]).reshape(slab_count, SLAB)
    slab_match = slab_order[:, None] == jnp.arange(slab_count, dtype=jnp.int32)[None, :]
    target = jnp.sum(jnp.where(slab_match[:, :, None], next_ids[None], 0), axis=1).reshape(-1)
    position = (slab_order[:, None] * SLAB + jnp.arange(SLAB, dtype=jnp.int32)).reshape(-1)
    has_target = position < seq_length - 1
    local_target = target - lax.axis_index("exp") * vocab_width
    weighting = jnp.where(has_target, weights, 0.0)
    columns = jnp.arange(vocab_width, dtype=jnp.int32)[None, :]
    per_row = jnp.stack([row_max, row_total, weighting, local_target.astype(jnp.float32)])

    def upstream_block(q, per_row, block_logits=None):
        count = seq_length // NY
        if block_logits is None:
            block_logits = rows_at(all_logits, q, count)
        top, total, weight, aim = lax.dynamic_slice_in_dim(per_row, q * count, count, axis=1)
        is_target = columns == aim.astype(jnp.int32)[:, None]
        logit_grads = (
            weight[:, None]
            * (
                jnp.exp(block_logits.astype(jnp.float32) - top[:, None])
                / total[:, None]
                - is_target.astype(jnp.float32)
            )
        ).astype(jnp.bfloat16)
        partial = jnp.dot(logit_grads, head_weight, preferred_element_type=jnp.float32)
        return (partial * 4096.0).astype(jnp.float16)

    far_index = (lax.axis_index("exp") // NZ + 2) % NY
    far_logits = lax.optimization_barrier(rows_at(all_logits, far_index, seq_length // NY))
    far_logits, per_row = lax.optimization_barrier((far_logits, per_row))
    far = upstream_block(far_index, per_row, far_logits)
    part_both = jnp.concatenate(
        [
            jnp.dot(flat_inputs, weight, preferred_element_type=jnp.float32).astype(jnp.float16)
            for weight in (gate_w, up_w)
        ],
        axis=1,
    )
    both_sum, far = ctx_scatter(part_both, far)
    over_y = ring_sum_over_y(upstream_block, far, per_row)
    upstream = exchange_sum(over_y, "exp", Z_GROUPS, NZ) * (1.0 / 4096.0)
    upstream_sent = upstream.astype(jnp.bfloat16)

    send_upstream = jnp.dot(slot_owner, upstream_sent, preferred_element_type=jnp.float32).astype(
        jnp.bfloat16
    )
    flat_upstream = exchange(send_upstream, "exp")
    flat_upstream, both_sum = lax.optimization_barrier((flat_upstream, both_sum))
    part_back = lax.dot_general(
        flat_upstream, down_w, CONTRACT_LAST, preferred_element_type=jnp.float32
    )
    back_sum, _ = ctx_scatter(part_back)

    hidden = w_gate.shape[2]
    own_count = slot_count // ctx_count
    ctx_index = lax.axis_index("ctx")
    own_prob = rows_at(flat_prob, ctx_index % 2 * 4 + ctx_index // 2, own_count)
    gate_grad, up_grad, prob_grad = unit_backward(
        both_sum[:, :hidden], both_sum[:, hidden:], back_sum, own_prob
    )
    prob_high, prob_low = split_high(prob_grad)
    lane = jnp.arange(128, dtype=jnp.int32)[None, :]
    prob_block = jnp.where(
        lane == 0, prob_high[:, None], jnp.where(lane == 1, prob_low[:, None], 0)
    ).astype(jnp.bfloat16)
    grads = ctx_gather(jnp.concatenate([gate_grad, up_grad, prob_block], axis=1))
    input_grad = lax.dot_general(
        grads[:, :hidden], gate_w, CONTRACT_LAST, preferred_element_type=jnp.float32
    ) + lax.dot_general(
        grads[:, hidden : 2 * hidden], up_w, CONTRACT_LAST, preferred_element_type=jnp.float32
    )
    back = exchange(
        jnp.concatenate([input_grad.astype(jnp.bfloat16), grads[:, 2 * hidden :]], axis=1), "exp"
    )
    d_x = upstream + lax.dot_general(
        slot_owner,
        back[:, :feature_width],
        (((0,), (0,)), ((), ())),
        preferred_element_type=jnp.float32,
    )
    d_prob = jnp.sum(
        lax.dot_general(
            back[:, feature_width : feature_width + 2],
            chosen.astype(jnp.bfloat16),
            (((0,), (0,)), ((), ())),
            preferred_element_type=jnp.float32,
        ),
        axis=0,
    ).reshape(token_count, route_count)
    return (d_x, d_prob)


def solution(mesh):
    placed = (
        P("ctx", "exp"),
        P("exp", "ctx"),
        P("ctx"),
        P(),
        P("ctx"),
        P("exp", "ctx"),
        P("exp", None),
        P("exp", None),
        P("exp", "ctx", None),
        P("exp", "ctx", None),
        P("exp", None, "ctx"),
    )
    return jax.shard_map(
        local,
        mesh=mesh,
        in_specs=placed,
        out_specs=(P("exp", "ctx"), P("exp", None)),
        check_vma=False,
    )
```

```python
import jax
import jax.numpy as jnp
from jax import lax
from jax.sharding import PartitionSpec as P

SLAB = 64
NY, NZ = 4, 8
Z_GROUPS = [[y * NZ + z for z in range(NZ)] for y in range(NY)]
CONTRACT_LAST = (((1,), (1,)), ((), ()))


def exchange(x, axis, groups=None):
    return lax.all_to_all(x, axis, 0, 0, tiled=True, axis_index_groups=groups)


def exchange_sum(x, axis, groups, parts):
    rows, width = x.shape
    got = exchange(x, axis, groups).reshape(parts, rows // parts, width)
    return jnp.sum(got.astype(jnp.float32), axis=0)


def split_high(x):
    high = lax.reduce_precision(x, 8, 7)
    return high, x - high


def ctx_shift(x, shift):
    return lax.ppermute(x, "ctx", [(i, (i + 2 * shift) % 8) for i in range(8)])


def ctx_swap(x):
    return lax.ppermute(x, "ctx", [(i, i ^ 1) for i in range(8)])


def rows_at(x, index, count):
    return lax.dynamic_slice_in_dim(x, index * count, count, axis=0)


def half_sum_over_ctx(x, after=None):
    core = lax.axis_index("ctx") % 2
    chip = lax.axis_index("ctx") // 2
    half_rows = x.shape[0] // 2
    own_rows = half_rows // 4
    x = x.astype(jnp.float16)
    other = ctx_swap(rows_at(x, 1 - core, half_rows))
    pair = (
        rows_at(x, core, half_rows).astype(jnp.float32) + other.astype(jnp.float32)
    ).astype(jnp.float16)
    if after is not None:
        pair, after = lax.optimization_barrier((pair, after))
    got = [ctx_shift(rows_at(pair, (chip + shift) % 4, own_rows), shift) for shift in (1, 3, 2)]
    own = rows_at(pair, chip, own_rows).astype(jnp.float32)
    for piece in got:
        own = own + piece.astype(jnp.float32)
    own = own.astype(jnp.float16)
    from_one, from_three, from_two = [ctx_shift(own, shift) for shift in (1, 3, 2)]
    half = jnp.zeros((half_rows, x.shape[1]), jnp.float16)
    for piece, shift in ((own, 0), (from_one, 1), (from_three, 3), (from_two, 2)):
        half = lax.dynamic_update_slice_in_dim(half, piece, (chip + 4 - shift) % 4 * own_rows, axis=0)
    return half, after


def both_halves(half):
    core = lax.axis_index("ctx") % 2
    other = ctx_swap(half)
    first = jnp.where(core == 0, half, other)
    second = jnp.where(core == 0, other, half)
    return jnp.concatenate([first, second], axis=0)


def y_shift(x, shift):
    return lax.ppermute(
        x, "exp", [(i, (i + NZ * shift) % (NY * NZ)) for i in range(NY * NZ)]
    )


def ring_sum_over_y(block, far, per_row):
    y = lax.axis_index("exp") // NZ
    split = far.shape[0] // 2
    from_down = y_shift(far[:split], 1)
    from_up = y_shift(far[split:], 3)
    up = block((y + 1) % NY, per_row)
    up_late = y_shift(up[split:], 1)
    down = block((y + 3) % NY, per_row)
    down_late = y_shift(down[:split], 3)
    up_sum = (up[:split].astype(jnp.float32) + from_down.astype(jnp.float32)).astype(up.dtype)
    up_sum = y_shift(up_sum, 1)
    down_sum = (down[split:].astype(jnp.float32) + from_up.astype(jnp.float32)).astype(up.dtype)
    down_sum = y_shift(down_sum, 3)
    own = block(y, per_row).astype(jnp.float32)
    first = own[:split] + up_sum.astype(jnp.float32) + down_late.astype(jnp.float32)
    second = own[split:] + up_late.astype(jnp.float32) + down_sum.astype(jnp.float32)
    return jnp.concatenate([first, second], axis=0).astype(up.dtype)


def unit_backward(gate_sum, up_sum, back_sum, slot_prob):
    gate_sigmoid = jax.nn.sigmoid(gate_sum)
    gate_silu = gate_sum * gate_sigmoid
    prob_part = jnp.sum(gate_silu * up_sum * back_sum, axis=1)
    scaled_back = slot_prob[:, None] * back_sum
    gate_grad = (
        scaled_back * up_sum * gate_sigmoid * (1.0 + gate_sum * (1.0 - gate_sigmoid))
    ).astype(jnp.bfloat16)
    up_grad = (scaled_back * gate_silu).astype(jnp.bfloat16)
    return (gate_grad, up_grad, prob_part)


def local(
    logits,
    head_weight,
    token_ids,
    slab_order,
    token_weights,
    moe_input,
    routes,
    probs,
    w_gate,
    w_up,
    w_down,
):
    ctx_count = lax.axis_size("ctx")
    exp_count = lax.axis_size("exp")
    row_count, vocab_width = logits.shape
    seq_length = row_count * ctx_count
    all_logits = lax.all_gather(logits, "ctx", axis=0, tiled=True)

    token_count, route_count = routes.shape
    feature_width = moe_input.shape[1]
    capacity = min(token_count, 2 * token_count * route_count // exp_count)
    slot_count = exp_count * capacity
    tokens = jnp.arange(token_count, dtype=jnp.int32)
    named = routes[:, :, None] == jnp.arange(exp_count, dtype=jnp.int32)[None, None, :]
    named_once = jnp.sum(named.astype(jnp.float32), axis=1)
    earlier = (tokens[:, None] > tokens[None, :]).astype(jnp.bfloat16)
    place = jnp.dot(
        earlier, named_once.astype(jnp.bfloat16), preferred_element_type=jnp.float32
    )
    place = jnp.where(named_once > 0, place, -1.0).T
    held = place[:, None, :] == jnp.arange(capacity, dtype=jnp.float32)[None, :, None]
    slot_owner = held.astype(jnp.bfloat16).reshape(slot_count, token_count)

    scores = logits.astype(jnp.float32)
    local_max = jnp.max(scores, axis=1)
    local_sum = jnp.sum(jnp.exp(scores - local_max[:, None]), axis=1)
    expert_prob = jnp.sum(jnp.where(named, probs.astype(jnp.float32)[:, :, None], 0.0), axis=1).T
    send_prob = jnp.sum(jnp.where(held, expert_prob[:, None, :], 0.0), axis=2).astype(jnp.bfloat16)
    send_input = jnp.dot(slot_owner, moe_input, preferred_element_type=jnp.float32).astype(
        jnp.bfloat16
    )
    sum_high, sum_rest = split_high(local_sum)
    sum_mid, sum_low = split_high(sum_rest)
    stats = jnp.stack([local_max, sum_high, sum_mid, sum_low]).astype(jnp.bfloat16)
    extra = jnp.concatenate(
        [
            jnp.broadcast_to(stats[None], (exp_count, 4, row_count)),
            jnp.pad(
                send_prob.reshape(exp_count, 1, capacity),
                ((0, 0), (0, capacity - 5), (0, row_count - capacity)),
            ),
        ],
        axis=1,
    ).reshape(slot_count, row_count)
    got = exchange(jnp.concatenate([send_input, extra], axis=1), "exp")
    flat_inputs = got[:, :feature_width]
    extra = got[:, feature_width:].reshape(exp_count, capacity, row_count)
    flat_prob = extra[:, 4, :capacity].reshape(-1).astype(jnp.float32)
    stats = extra[:, :4].astype(jnp.float32)
    all_max = stats[:, 0]
    row_max = jnp.max(all_max, axis=0)
    row_total = jnp.sum(
        (stats[:, 1] + stats[:, 2] + stats[:, 3]) * jnp.exp(all_max - row_max), axis=0
    )
    rows = jnp.concatenate([row_max, row_total, token_weights, token_ids.astype(jnp.float32)])
    rows = exchange(jnp.broadcast_to(rows[None], (ctx_count, 4 * row_count)), "ctx")
    rows = rows.reshape(ctx_count, 4, row_count).transpose(1, 0, 2).reshape(4, seq_length)
    rows, all_logits = lax.optimization_barrier((rows, all_logits))

    gate_w = w_gate[0]
    up_w = w_up[0]
    down_w = w_down[0]
    row_max, row_total, weights = rows[0], rows[1], rows[2]
    all_ids = rows[3].astype(jnp.int32)

    one = 1 - jnp.minimum(lax.axis_index("ctx"), 0)
    head_weight = lax.optimization_barrier(head_weight * one.astype(jnp.bfloat16))

    slab_count = slab_order.shape[0]
    next_ids = jnp.concatenate([all_ids[1:], all_ids[-1:]]).reshape(slab_count, SLAB)
    slab_match = slab_order[:, None] == jnp.arange(slab_count, dtype=jnp.int32)[None, :]
    target = jnp.sum(jnp.where(slab_match[:, :, None], next_ids[None], 0), axis=1).reshape(-1)
    position = (slab_order[:, None] * SLAB + jnp.arange(SLAB, dtype=jnp.int32)).reshape(-1)
    has_target = position < seq_length - 1
    local_target = target - lax.axis_index("exp") * vocab_width
    weighting = jnp.where(has_target, weights, 0.0)
    columns = jnp.arange(vocab_width, dtype=jnp.int32)[None, :]
    per_row = jnp.stack([row_max, row_total, weighting, local_target.astype(jnp.float32)])

    def upstream_block(q, per_row):
        count = seq_length // NY
        top, total, weight, aim = lax.dynamic_slice_in_dim(per_row, q * count, count, axis=1)
        is_target = columns == aim.astype(jnp.int32)[:, None]
        logit_grads = (
            weight[:, None]
            * (
                jnp.exp(rows_at(all_logits, q, count).astype(jnp.float32) - top[:, None])
                / total[:, None]
                - is_target.astype(jnp.float32)
            )
        ).astype(jnp.bfloat16)
        partial = jnp.dot(logit_grads, head_weight, preferred_element_type=jnp.float32)
        return (partial * 4096.0).astype(jnp.float16)

    far = upstream_block((lax.axis_index("exp") // NZ + 2) % NY, per_row)
    far, flat_inputs = lax.optimization_barrier((far, flat_inputs))
    over_y = ring_sum_over_y(upstream_block, far, per_row)
    part_both = jnp.concatenate(
        [
            jnp.dot(flat_inputs, weight, preferred_element_type=jnp.float32).astype(jnp.float16)
            for weight in (gate_w, up_w)
        ],
        axis=1,
    )
    over_y, part_both = lax.optimization_barrier((over_y, part_both))
    upstream = exchange_sum(over_y, "exp", Z_GROUPS, NZ) * (1.0 / 4096.0)
    both_sum, upstream = half_sum_over_ctx(part_both, upstream)
    upstream_sent = upstream.astype(jnp.bfloat16)

    send_upstream = jnp.dot(slot_owner, upstream_sent, preferred_element_type=jnp.float32).astype(
        jnp.bfloat16
    )
    flat_upstream = exchange(send_upstream, "exp")
    flat_upstream, both_sum = lax.optimization_barrier((flat_upstream, both_sum))
    part_back = lax.dot_general(
        flat_upstream, down_w, CONTRACT_LAST, preferred_element_type=jnp.float32
    )
    back_sum, _ = half_sum_over_ctx(part_back)

    hidden = w_gate.shape[2]
    both_sum = both_sum.astype(jnp.float32)
    core_prob = rows_at(flat_prob, lax.axis_index("ctx") % 2, slot_count // 2)
    gate_grad, up_grad, prob_grad = unit_backward(
        both_sum[:, :hidden], both_sum[:, hidden:], back_sum.astype(jnp.float32), core_prob
    )
    prob_high, prob_low = split_high(prob_grad)
    lane = jnp.arange(128, dtype=jnp.int32)[None, :]
    prob_block = jnp.where(
        lane == 0, prob_high[:, None], jnp.where(lane == 1, prob_low[:, None], 0)
    ).astype(jnp.bfloat16)
    grads = both_halves(jnp.concatenate([gate_grad, up_grad, prob_block], axis=1))
    input_grad = lax.dot_general(
        grads[:, :hidden], gate_w, CONTRACT_LAST, preferred_element_type=jnp.float32
    ) + lax.dot_general(
        grads[:, hidden : 2 * hidden], up_w, CONTRACT_LAST, preferred_element_type=jnp.float32
    )
    back = exchange(
        jnp.concatenate([input_grad.astype(jnp.bfloat16), grads[:, 2 * hidden :]], axis=1), "exp"
    )
    d_x = upstream + lax.dot_general(
        slot_owner,
        back[:, :feature_width],
        (((0,), (0,)), ((), ())),
        preferred_element_type=jnp.float32,
    )
    back_prob = back[:, feature_width : feature_width + 2].astype(jnp.float32)
    back_prob = (back_prob[:, 0] + back_prob[:, 1]).reshape(exp_count, capacity)
    token_prob = jnp.sum(jnp.where(held, back_prob[:, :, None], 0.0), axis=1).T
    d_prob = jnp.sum(jnp.where(named, token_prob[:, None, :], 0.0), axis=2)
    return (d_x, d_prob)


def solution(mesh):
    placed = (
        P("ctx", "exp"),
        P("exp", "ctx"),
        P("ctx"),
        P(),
        P("ctx"),
        P("exp", "ctx"),
        P("exp", None),
        P("exp", None),
        P("exp", "ctx", None),
        P("exp", "ctx", None),
        P("exp", None, "ctx"),
    )
    return jax.shard_map(
        local,
        mesh=mesh,
        in_specs=placed,
        out_specs=(P("exp", "ctx"), P("exp", None)),
        check_vma=False,
    )
```

```python
import jax
import jax.numpy as jnp
from jax import lax
from jax.sharding import PartitionSpec as P

SLAB = 64
NY, NZ = 4, 8
Z_GROUPS = [[y * NZ + z for z in range(NZ)] for y in range(NY)]
CONTRACT_LAST = (((1,), (1,)), ((), ()))


def exchange(x, axis, groups=None):
    return lax.all_to_all(x, axis, 0, 0, tiled=True, axis_index_groups=groups)


def exchange_sum(x, axis, groups, parts):
    rows, width = x.shape
    got = exchange(x, axis, groups).reshape(parts, rows // parts, width)
    return jnp.sum(got.astype(jnp.float32), axis=0)


def split_high(x):
    high = lax.reduce_precision(x, 8, 7)
    return high, x - high


def ctx_shift(x, shift):
    return lax.ppermute(x, "ctx", [(i, (i + 2 * shift) % 8) for i in range(8)])


def ctx_swap(x):
    return lax.ppermute(x, "ctx", [(i, i ^ 1) for i in range(8)])


def rows_at(x, index, count):
    return lax.dynamic_slice_in_dim(x, index * count, count, axis=0)


def ctx_scatter(x):
    core = lax.axis_index("ctx") % 2
    chip = lax.axis_index("ctx") // 2
    half_rows = x.shape[0] // 2
    own_rows = half_rows // 4
    x = x.astype(jnp.float16)
    other = ctx_swap(rows_at(x, 1 - core, half_rows))
    pair = (
        rows_at(x, core, half_rows).astype(jnp.float32) + other.astype(jnp.float32)
    ).astype(jnp.float16)
    got = [ctx_shift(rows_at(pair, (chip + shift) % 4, own_rows), shift) for shift in (1, 3, 2)]
    own = rows_at(pair, chip, own_rows).astype(jnp.float32)
    for piece in got:
        own = own + piece.astype(jnp.float32)
    return own


def ctx_gather(own):
    core = lax.axis_index("ctx") % 2
    chip = lax.axis_index("ctx") // 2
    own_rows, width = own.shape
    from_one, from_three, from_two = [ctx_shift(own, shift) for shift in (1, 3, 2)]
    half = jnp.zeros((4 * own_rows, width), own.dtype)
    for piece, shift in ((own, 0), (from_one, 1), (from_three, 3), (from_two, 2)):
        half = lax.dynamic_update_slice_in_dim(half, piece, (chip + 4 - shift) % 4 * own_rows, axis=0)
    other = ctx_swap(half)
    first = jnp.where(core == 0, half, other)
    second = jnp.where(core == 0, other, half)
    return jnp.concatenate([first, second], axis=0)


def y_shift(x, shift):
    return lax.ppermute(
        x, "exp", [(i, (i + NZ * shift) % (NY * NZ)) for i in range(NY * NZ)]
    )


def ring_sum_over_y(block, far, per_row):
    y = lax.axis_index("exp") // NZ
    split = far.shape[0] // 2
    from_down = y_shift(far[:split], 1)
    from_up = y_shift(far[split:], 3)
    up = block((y + 1) % NY, per_row)
    up_late = y_shift(up[split:], 1)
    down = block((y + 3) % NY, per_row)
    down_late = y_shift(down[:split], 3)
    up_sum = (up[:split].astype(jnp.float32) + from_down.astype(jnp.float32)).astype(up.dtype)
    up_sum = y_shift(up_sum, 1)
    down_sum = (down[split:].astype(jnp.float32) + from_up.astype(jnp.float32)).astype(up.dtype)
    down_sum = y_shift(down_sum, 3)
    own = block(y, per_row).astype(jnp.float32)
    first = own[:split] + up_sum.astype(jnp.float32) + down_late.astype(jnp.float32)
    second = own[split:] + up_late.astype(jnp.float32) + down_sum.astype(jnp.float32)
    return jnp.concatenate([first, second], axis=0).astype(up.dtype)


def unit_backward(gate_sum, up_sum, back_sum, slot_prob):
    gate_sigmoid = jax.nn.sigmoid(gate_sum)
    gate_silu = gate_sum * gate_sigmoid
    prob_part = jnp.sum(gate_silu * up_sum * back_sum, axis=1)
    scaled_back = slot_prob[:, None] * back_sum
    gate_grad = (
        scaled_back * up_sum * gate_sigmoid * (1.0 + gate_sum * (1.0 - gate_sigmoid))
    ).astype(jnp.bfloat16)
    up_grad = (scaled_back * gate_silu).astype(jnp.bfloat16)
    return (gate_grad, up_grad, prob_part)


def local(
    logits,
    head_weight,
    token_ids,
    slab_order,
    token_weights,
    moe_input,
    routes,
    probs,
    w_gate,
    w_up,
    w_down,
):
    ctx_count = lax.axis_size("ctx")
    exp_count = lax.axis_size("exp")
    row_count, vocab_width = logits.shape
    seq_length = row_count * ctx_count
    all_logits = lax.all_gather(logits, "ctx", axis=0, tiled=True)

    token_count, route_count = routes.shape
    feature_width = moe_input.shape[1]
    capacity = min(token_count, 2 * token_count * route_count // exp_count)
    slot_count = exp_count * capacity
    tokens = jnp.arange(token_count, dtype=jnp.int32)
    experts = jnp.arange(exp_count, dtype=jnp.int32)
    named = routes.T[None] == experts[:, None, None]
    named_once = jnp.sum(named.astype(jnp.float32), axis=1)
    earlier = (tokens[:, None] < tokens[None, :]).astype(jnp.bfloat16)
    place = jnp.dot(named_once.astype(jnp.bfloat16), earlier, preferred_element_type=jnp.float32)
    place = jnp.where(named_once > 0, place, -1.0)
    held = place[:, None, :] == jnp.arange(capacity, dtype=jnp.float32)[None, :, None]
    slot_owner = held.astype(jnp.bfloat16).reshape(slot_count, token_count)

    scores = logits.astype(jnp.float32)
    local_max = jnp.max(scores, axis=1)
    local_sum = jnp.sum(jnp.exp(scores - local_max[:, None]), axis=1)
    expert_prob = jnp.sum(jnp.where(named, probs.astype(jnp.float32).T[None], 0.0), axis=1)
    send_prob = jnp.sum(jnp.where(held, expert_prob[:, None, :], 0.0), axis=2).astype(jnp.bfloat16)
    send_input = jnp.dot(slot_owner, moe_input, preferred_element_type=jnp.float32).astype(
        jnp.bfloat16
    )
    sum_high, sum_rest = split_high(local_sum)
    sum_mid, sum_low = split_high(sum_rest)
    stats = jnp.stack([local_max, sum_high, sum_mid, sum_low]).astype(jnp.bfloat16)
    extra = jnp.concatenate(
        [
            jnp.broadcast_to(stats[None], (exp_count, 4, row_count)),
            jnp.pad(
                send_prob.reshape(exp_count, 1, capacity),
                ((0, 0), (0, capacity - 5), (0, row_count - capacity)),
            ),
        ],
        axis=1,
    ).reshape(slot_count, row_count)
    got = exchange(jnp.concatenate([send_input, extra], axis=1), "exp")
    flat_inputs = got[:, :feature_width]
    extra = got[:, feature_width:].reshape(exp_count, capacity, row_count)
    flat_prob = extra[:, 4, :capacity].reshape(-1).astype(jnp.float32)
    stats = extra[:, :4].astype(jnp.float32)
    all_max = stats[:, 0]
    row_max = jnp.max(all_max, axis=0)
    row_total = jnp.sum(
        (stats[:, 1] + stats[:, 2] + stats[:, 3]) * jnp.exp(all_max - row_max), axis=0
    )
    rows = jnp.concatenate([row_max, row_total, token_weights, token_ids.astype(jnp.float32)])
    rows, head_weight = lax.optimization_barrier((rows, head_weight))
    rows = exchange(jnp.broadcast_to(rows[None], (ctx_count, 4 * row_count)), "ctx")
    rows = rows.reshape(ctx_count, 4, row_count).transpose(1, 0, 2).reshape(4, seq_length)
    rows, all_logits = lax.optimization_barrier((rows, all_logits))

    gate_w = w_gate[0]
    up_w = w_up[0]
    down_w = w_down[0]
    row_max, row_total, weights = rows[0], rows[1], rows[2]
    all_ids = rows[3].astype(jnp.int32)

    one = 1 - jnp.minimum(lax.axis_index("ctx"), 0)
    head_weight = lax.optimization_barrier(head_weight * one.astype(jnp.bfloat16))

    slab_count = slab_order.shape[0]
    next_ids = jnp.concatenate([all_ids[1:], all_ids[-1:]]).reshape(slab_count, SLAB)
    slab_match = slab_order[:, None] == jnp.arange(slab_count, dtype=jnp.int32)[None, :]
    target = jnp.sum(jnp.where(slab_match[:, :, None], next_ids[None], 0), axis=1).reshape(-1)
    position = (slab_order[:, None] * SLAB + jnp.arange(SLAB, dtype=jnp.int32)).reshape(-1)
    has_target = position < seq_length - 1
    local_target = target - lax.axis_index("exp") * vocab_width
    weighting = jnp.where(has_target, weights, 0.0)
    columns = jnp.arange(vocab_width, dtype=jnp.int32)[None, :]
    per_row = jnp.stack([row_max, row_total, weighting, local_target.astype(jnp.float32)])

    def upstream_block(q, per_row):
        count = seq_length // NY
        top, total, weight, aim = lax.dynamic_slice_in_dim(per_row, q * count, count, axis=1)
        is_target = columns == aim.astype(jnp.int32)[:, None]
        logit_grads = (
            weight[:, None]
            * (
                jnp.exp(rows_at(all_logits, q, count).astype(jnp.float32) - top[:, None])
                / total[:, None]
                - is_target.astype(jnp.float32)
            )
        ).astype(jnp.bfloat16)
        partial = jnp.dot(logit_grads, head_weight, preferred_element_type=jnp.float32)
        return (partial * 4096.0).astype(jnp.float16)

    far = upstream_block((lax.axis_index("exp") // NZ + 2) % NY, per_row)
    far, flat_inputs = lax.optimization_barrier((far, flat_inputs))
    over_y = ring_sum_over_y(upstream_block, far, per_row)
    part_both = jnp.concatenate(
        [
            jnp.dot(flat_inputs, weight, preferred_element_type=jnp.float32).astype(jnp.float16)
            for weight in (gate_w, up_w)
        ],
        axis=1,
    )
    both_sum = ctx_scatter(part_both)
    upstream = exchange_sum(over_y, "exp", Z_GROUPS, NZ) * (1.0 / 4096.0)
    upstream_sent = upstream.astype(jnp.bfloat16)

    send_upstream = jnp.dot(slot_owner, upstream_sent, preferred_element_type=jnp.float32).astype(
        jnp.bfloat16
    )
    flat_upstream = exchange(send_upstream, "exp")
    flat_upstream, both_sum = lax.optimization_barrier((flat_upstream, both_sum))
    part_back = lax.dot_general(
        flat_upstream, down_w, CONTRACT_LAST, preferred_element_type=jnp.float32
    )
    back_sum = ctx_scatter(part_back)

    hidden = w_gate.shape[2]
    own_count = slot_count // ctx_count
    ctx_index = lax.axis_index("ctx")
    own_prob = rows_at(flat_prob, ctx_index % 2 * 4 + ctx_index // 2, own_count)
    gate_grad, up_grad, prob_grad = unit_backward(
        both_sum[:, :hidden], both_sum[:, hidden:], back_sum, own_prob
    )
    prob_high, prob_low = split_high(prob_grad)
    lane = jnp.arange(128, dtype=jnp.int32)[None, :]
    prob_block = jnp.where(
        lane == 0, prob_high[:, None], jnp.where(lane == 1, prob_low[:, None], 0)
    ).astype(jnp.bfloat16)
    grads = ctx_gather(jnp.concatenate([gate_grad, up_grad, prob_block], axis=1))
    input_grad = lax.dot_general(
        grads[:, :hidden], gate_w, CONTRACT_LAST, preferred_element_type=jnp.float32
    ) + lax.dot_general(
        grads[:, hidden : 2 * hidden], up_w, CONTRACT_LAST, preferred_element_type=jnp.float32
    )
    back = exchange(
        jnp.concatenate([input_grad.astype(jnp.bfloat16), grads[:, 2 * hidden :]], axis=1), "exp"
    )
    d_x = upstream + lax.dot_general(
        slot_owner,
        back[:, :feature_width],
        (((0,), (0,)), ((), ())),
        preferred_element_type=jnp.float32,
    )
    back_prob = back[:, feature_width : feature_width + 2].astype(jnp.float32)
    back_prob = (back_prob[:, 0] + back_prob[:, 1]).reshape(exp_count, capacity)
    token_prob = jnp.sum(jnp.where(held, back_prob[:, :, None], 0.0), axis=1)
    d_prob = jnp.sum(jnp.where(named, token_prob[:, None, :], 0.0), axis=0).T
    return (d_x, d_prob)


def solution(mesh):
    placed = (
        P("ctx", "exp"),
        P("exp", "ctx"),
        P("ctx"),
        P(),
        P("ctx"),
        P("exp", "ctx"),
        P("exp", None),
        P("exp", None),
        P("exp", "ctx", None),
        P("exp", "ctx", None),
        P("exp", None, "ctx"),
    )
    return jax.shard_map(
        local,
        mesh=mesh,
        in_specs=placed,
        out_specs=(P("exp", "ctx"), P("exp", None)),
        check_vma=False,
    )
```

```python
import jax
import jax.numpy as jnp
from jax import lax
from jax.sharding import PartitionSpec as P

SLAB = 64
NY, NZ = 4, 8
Z_GROUPS = [[y * NZ + z for z in range(NZ)] for y in range(NY)]
CONTRACT_LAST = (((1,), (1,)), ((), ()))


def exchange(x, axis, groups=None):
    return lax.all_to_all(x, axis, 0, 0, tiled=True, axis_index_groups=groups)


def exchange_sum(x, axis, groups, parts):
    rows, width = x.shape
    got = exchange(x, axis, groups).reshape(parts, rows // parts, width)
    return jnp.sum(got.astype(jnp.float32), axis=0)


def split_high(x):
    high = lax.reduce_precision(x, 8, 7)
    return high, x - high


def ctx_shift(x, shift):
    return lax.ppermute(x, "ctx", [(i, (i + 2 * shift) % 8) for i in range(8)])


def ctx_swap(x):
    return lax.ppermute(x, "ctx", [(i, i ^ 1) for i in range(8)])


def rows_at(x, index, count):
    return lax.dynamic_slice_in_dim(x, index * count, count, axis=0)


def ctx_scatter(x):
    core = lax.axis_index("ctx") % 2
    chip = lax.axis_index("ctx") // 2
    half_rows = x.shape[0] // 2
    own_rows = half_rows // 4
    x = x.astype(jnp.float16)
    other = ctx_swap(rows_at(x, 1 - core, half_rows))
    pair = (
        rows_at(x, core, half_rows).astype(jnp.float32) + other.astype(jnp.float32)
    ).astype(jnp.float16)
    got = [ctx_shift(rows_at(pair, (chip + shift) % 4, own_rows), shift) for shift in (1, 3, 2)]
    own = rows_at(pair, chip, own_rows).astype(jnp.float32)
    for piece in got:
        own = own + piece.astype(jnp.float32)
    return own


def ctx_gather(own):
    core = lax.axis_index("ctx") % 2
    chip = lax.axis_index("ctx") // 2
    own_rows, width = own.shape
    from_one, from_three, from_two = [ctx_shift(own, shift) for shift in (1, 3, 2)]
    half = jnp.zeros((4 * own_rows, width), own.dtype)
    for piece, shift in ((own, 0), (from_one, 1), (from_three, 3), (from_two, 2)):
        half = lax.dynamic_update_slice_in_dim(half, piece, (chip + 4 - shift) % 4 * own_rows, axis=0)
    other = ctx_swap(half)
    first = jnp.where(core == 0, half, other)
    second = jnp.where(core == 0, other, half)
    return jnp.concatenate([first, second], axis=0)


def y_shift(x, shift):
    return lax.ppermute(
        x, "exp", [(i, (i + NZ * shift) % (NY * NZ)) for i in range(NY * NZ)]
    )


def ring_sum_over_y(block, far, per_row):
    y = lax.axis_index("exp") // NZ
    split = far.shape[0] // 2
    from_down = y_shift(far[:split], 1)
    from_up = y_shift(far[split:], 3)
    up = block((y + 1) % NY, per_row)
    up_late = y_shift(up[split:], 1)
    down = block((y + 3) % NY, per_row)
    down_late = y_shift(down[:split], 3)
    up_sum = (up[:split].astype(jnp.float32) + from_down.astype(jnp.float32)).astype(up.dtype)
    up_sum = y_shift(up_sum, 1)
    down_sum = (down[split:].astype(jnp.float32) + from_up.astype(jnp.float32)).astype(up.dtype)
    down_sum = y_shift(down_sum, 3)
    own = block(y, per_row).astype(jnp.float32)
    first = own[:split] + up_sum.astype(jnp.float32) + down_late.astype(jnp.float32)
    second = own[split:] + up_late.astype(jnp.float32) + down_sum.astype(jnp.float32)
    return jnp.concatenate([first, second], axis=0).astype(up.dtype)


def unit_backward(gate_sum, up_sum, back_sum, slot_prob):
    gate_sigmoid = jax.nn.sigmoid(gate_sum)
    gate_silu = gate_sum * gate_sigmoid
    prob_part = jnp.sum(gate_silu * up_sum * back_sum, axis=1)
    scaled_back = slot_prob[:, None] * back_sum
    gate_grad = (
        scaled_back * up_sum * gate_sigmoid * (1.0 + gate_sum * (1.0 - gate_sigmoid))
    ).astype(jnp.bfloat16)
    up_grad = (scaled_back * gate_silu).astype(jnp.bfloat16)
    return (gate_grad, up_grad, prob_part)


def local(
    logits,
    head_weight,
    token_ids,
    slab_order,
    token_weights,
    moe_input,
    routes,
    probs,
    w_gate,
    w_up,
    w_down,
):
    ctx_count = lax.axis_size("ctx")
    exp_count = lax.axis_size("exp")
    row_count, vocab_width = logits.shape
    seq_length = row_count * ctx_count
    all_logits = lax.all_gather(logits, "ctx", axis=0, tiled=True)

    token_count, route_count = routes.shape
    feature_width = moe_input.shape[1]
    capacity = min(token_count, 2 * token_count * route_count // exp_count)
    slot_count = exp_count * capacity
    tokens = jnp.arange(token_count, dtype=jnp.int32)
    experts = jnp.arange(exp_count, dtype=jnp.int32)
    named = routes.T[None] == experts[:, None, None]
    named_once = jnp.sum(named.astype(jnp.float32), axis=1)
    earlier = (tokens[:, None] < tokens[None, :]).astype(jnp.bfloat16)
    place = jnp.dot(named_once.astype(jnp.bfloat16), earlier, preferred_element_type=jnp.float32)
    place = jnp.where(named_once > 0, place, -1.0)
    held = place[:, None, :] == jnp.arange(capacity, dtype=jnp.float32)[None, :, None]
    slot_owner = held.astype(jnp.bfloat16).reshape(slot_count, token_count)

    scores = logits.astype(jnp.float32)
    local_max = jnp.max(scores, axis=1)
    local_sum = jnp.sum(jnp.exp(scores - local_max[:, None]), axis=1)
    expert_prob = jnp.sum(jnp.where(named, probs.astype(jnp.float32).T[None], 0.0), axis=1)
    send_prob = jnp.sum(jnp.where(held, expert_prob[:, None, :], 0.0), axis=2).astype(jnp.bfloat16)
    send_input = jnp.dot(slot_owner, moe_input, preferred_element_type=jnp.float32).astype(
        jnp.bfloat16
    )
    sum_high, sum_rest = split_high(local_sum)
    sum_mid, sum_low = split_high(sum_rest)
    stats = jnp.stack([local_max, sum_high, sum_mid, sum_low]).astype(jnp.bfloat16)
    extra = jnp.concatenate(
        [
            jnp.broadcast_to(stats[None], (exp_count, 4, row_count)),
            jnp.pad(
                send_prob.reshape(exp_count, 1, capacity),
                ((0, 0), (0, capacity - 5), (0, row_count - capacity)),
            ),
        ],
        axis=1,
    ).reshape(slot_count, row_count)
    got = exchange(jnp.concatenate([send_input, extra], axis=1), "exp")
    flat_inputs = got[:, :feature_width]
    extra = got[:, feature_width:].reshape(exp_count, capacity, row_count)
    flat_prob = extra[:, 4, :capacity].reshape(-1).astype(jnp.float32)
    stats = extra[:, :4].astype(jnp.float32)
    all_max = stats[:, 0]
    row_max = jnp.max(all_max, axis=0)
    row_total = jnp.sum(
        (stats[:, 1] + stats[:, 2] + stats[:, 3]) * jnp.exp(all_max - row_max), axis=0
    )
    own_ids = token_ids.astype(jnp.float32)
    later_id = lax.ppermute(
        own_ids[:1], "ctx", [((i + 1) % ctx_count, i) for i in range(ctx_count)]
    )
    own_next = jnp.concatenate([own_ids[1:], later_id])
    rows = jnp.concatenate([row_max, row_total, token_weights, own_next])
    rows = exchange(jnp.broadcast_to(rows[None], (ctx_count, 4 * row_count)), "ctx")
    rows = rows.reshape(ctx_count, 4, row_count).transpose(1, 0, 2).reshape(4, seq_length)
    rows, all_logits = lax.optimization_barrier((rows, all_logits))

    gate_w = w_gate[0]
    up_w = w_up[0]
    down_w = w_down[0]
    row_max, row_total, weights = rows[0], rows[1], rows[2]
    all_next = rows[3].astype(jnp.int32)

    one = 1 - jnp.minimum(lax.axis_index("ctx"), 0)
    head_weight = lax.optimization_barrier(head_weight * one.astype(jnp.bfloat16))

    slab_count = slab_order.shape[0]
    next_ids = all_next.reshape(slab_count, SLAB)
    slab_match = slab_order[:, None] == jnp.arange(slab_count, dtype=jnp.int32)[None, :]
    target = jnp.sum(jnp.where(slab_match[:, :, None], next_ids[None], 0), axis=1).reshape(-1)
    position = (slab_order[:, None] * SLAB + jnp.arange(SLAB, dtype=jnp.int32)).reshape(-1)
    has_target = position < seq_length - 1
    local_target = target - lax.axis_index("exp") * vocab_width
    weighting = jnp.where(has_target, weights, 0.0)
    columns = jnp.arange(vocab_width, dtype=jnp.int32)[None, :]
    per_row = jnp.stack([row_max, row_total, weighting, local_target.astype(jnp.float32)])

    def upstream_block(q, per_row):
        count = seq_length // NY
        top, total, weight, aim = lax.dynamic_slice_in_dim(per_row, q * count, count, axis=1)
        is_target = columns == aim.astype(jnp.int32)[:, None]
        logit_grads = (
            weight[:, None]
            * (
                jnp.exp(rows_at(all_logits, q, count).astype(jnp.float32) - top[:, None])
                / total[:, None]
                - is_target.astype(jnp.float32)
            )
        ).astype(jnp.bfloat16)
        partial = jnp.dot(logit_grads, head_weight, preferred_element_type=jnp.float32)
        return (partial * 4096.0).astype(jnp.float16)

    far = upstream_block((lax.axis_index("exp") // NZ + 2) % NY, per_row)
    far, flat_inputs = lax.optimization_barrier((far, flat_inputs))
    over_y = ring_sum_over_y(upstream_block, far, per_row)
    part_both = jnp.concatenate(
        [
            jnp.dot(flat_inputs, weight, preferred_element_type=jnp.float32).astype(jnp.float16)
            for weight in (gate_w, up_w)
        ],
        axis=1,
    )
    both_sum = ctx_scatter(part_both)
    upstream = exchange_sum(over_y, "exp", Z_GROUPS, NZ) * (1.0 / 4096.0)
    upstream_sent = upstream.astype(jnp.bfloat16)

    send_upstream = jnp.dot(slot_owner, upstream_sent, preferred_element_type=jnp.float32).astype(
        jnp.bfloat16
    )
    flat_upstream = exchange(send_upstream, "exp")
    flat_upstream, both_sum = lax.optimization_barrier((flat_upstream, both_sum))
    part_back = lax.dot_general(
        flat_upstream, down_w, CONTRACT_LAST, preferred_element_type=jnp.float32
    )
    back_sum = ctx_scatter(part_back)

    hidden = w_gate.shape[2]
    own_count = slot_count // ctx_count
    ctx_index = lax.axis_index("ctx")
    own_prob = rows_at(flat_prob, ctx_index % 2 * 4 + ctx_index // 2, own_count)
    gate_grad, up_grad, prob_grad = unit_backward(
        both_sum[:, :hidden], both_sum[:, hidden:], back_sum, own_prob
    )
    prob_high, prob_low = split_high(prob_grad)
    lane = jnp.arange(128, dtype=jnp.int32)[None, :]
    prob_block = jnp.where(
        lane == 0, prob_high[:, None], jnp.where(lane == 1, prob_low[:, None], 0)
    ).astype(jnp.bfloat16)
    grads = ctx_gather(jnp.concatenate([gate_grad, up_grad, prob_block], axis=1))
    input_grad = lax.dot_general(
        grads[:, :hidden], gate_w, CONTRACT_LAST, preferred_element_type=jnp.float32
    ) + lax.dot_general(
        grads[:, hidden : 2 * hidden], up_w, CONTRACT_LAST, preferred_element_type=jnp.float32
    )
    back = exchange(
        jnp.concatenate([input_grad.astype(jnp.bfloat16), grads[:, 2 * hidden :]], axis=1), "exp"
    )
    d_x = upstream + lax.dot_general(
        slot_owner,
        back[:, :feature_width],
        (((0,), (0,)), ((), ())),
        preferred_element_type=jnp.float32,
    )
    back_prob = back[:, feature_width : feature_width + 2].astype(jnp.float32)
    back_prob = (back_prob[:, 0] + back_prob[:, 1]).reshape(exp_count, capacity)
    token_prob = jnp.sum(jnp.where(held, back_prob[:, :, None], 0.0), axis=1)
    d_prob = jnp.sum(jnp.where(named, token_prob[:, None, :], 0.0), axis=0).T
    return (d_x, d_prob)


def solution(mesh):
    placed = (
        P("ctx", "exp"),
        P("exp", "ctx"),
        P("ctx"),
        P(),
        P("ctx"),
        P("exp", "ctx"),
        P("exp", None),
        P("exp", None),
        P("exp", "ctx", None),
        P("exp", "ctx", None),
        P("exp", None, "ctx"),
    )
    return jax.shard_map(
        local,
        mesh=mesh,
        in_specs=placed,
        out_specs=(P("exp", "ctx"), P("exp", None)),
        check_vma=False,
    )
```

```python
import jax
import jax.numpy as jnp
from jax import lax
from jax.sharding import PartitionSpec as P

SLAB = 64
NY, NZ = 4, 8
Z_GROUPS = [[y * NZ + z for z in range(NZ)] for y in range(NY)]
CONTRACT_LAST = (((1,), (1,)), ((), ()))


def exchange(x, axis, groups=None):
    return lax.all_to_all(x, axis, 0, 0, tiled=True, axis_index_groups=groups)


def exchange_sum(x, axis, groups, parts):
    rows, width = x.shape
    got = exchange(x, axis, groups).reshape(parts, rows // parts, width)
    return jnp.sum(got.astype(jnp.float32), axis=0)


def split_high(x):
    high = lax.reduce_precision(x, 8, 7)
    return high, x - high


def ctx_shift(x, shift):
    return lax.ppermute(x, "ctx", [(i, (i + 2 * shift) % 8) for i in range(8)])


def ctx_swap(x):
    return lax.ppermute(x, "ctx", [(i, i ^ 1) for i in range(8)])


def rows_at(x, index, count):
    return lax.dynamic_slice_in_dim(x, index * count, count, axis=0)


def ctx_scatter(x):
    core = lax.axis_index("ctx") % 2
    chip = lax.axis_index("ctx") // 2
    half_rows = x.shape[0] // 2
    own_rows = half_rows // 4
    x = x.astype(jnp.float16)
    other = ctx_swap(rows_at(x, 1 - core, half_rows))
    pair = (
        rows_at(x, core, half_rows).astype(jnp.float32) + other.astype(jnp.float32)
    ).astype(jnp.float16)
    got = [ctx_shift(rows_at(pair, (chip + shift) % 4, own_rows), shift) for shift in (1, 3, 2)]
    own = rows_at(pair, chip, own_rows).astype(jnp.float32)
    for piece in got:
        own = own + piece.astype(jnp.float32)
    return own


def chips_gather(own):
    chip = lax.axis_index("ctx") // 2
    own_rows, width = own.shape
    from_one, from_three, from_two = [ctx_shift(own, shift) for shift in (1, 3, 2)]
    half = jnp.zeros((4 * own_rows, width), own.dtype)
    for piece, shift in ((own, 0), (from_one, 1), (from_three, 3), (from_two, 2)):
        half = lax.dynamic_update_slice_in_dim(half, piece, (chip + 4 - shift) % 4 * own_rows, axis=0)
    return half


def y_shift(x, shift):
    return lax.ppermute(
        x, "exp", [(i, (i + NZ * shift) % (NY * NZ)) for i in range(NY * NZ)]
    )


def ring_sum_over_y(block, far, per_row):
    y = lax.axis_index("exp") // NZ
    split = far.shape[0] // 2
    from_down = y_shift(far[:split], 1)
    from_up = y_shift(far[split:], 3)
    up = block((y + 1) % NY, per_row)
    up_late = y_shift(up[split:], 1)
    down = block((y + 3) % NY, per_row)
    down_late = y_shift(down[:split], 3)
    up_sum = (up[:split].astype(jnp.float32) + from_down.astype(jnp.float32)).astype(up.dtype)
    up_sum = y_shift(up_sum, 1)
    down_sum = (down[split:].astype(jnp.float32) + from_up.astype(jnp.float32)).astype(up.dtype)
    down_sum = y_shift(down_sum, 3)
    own = block(y, per_row).astype(jnp.float32)
    first = own[:split] + up_sum.astype(jnp.float32) + down_late.astype(jnp.float32)
    second = own[split:] + up_late.astype(jnp.float32) + down_sum.astype(jnp.float32)
    return jnp.concatenate([first, second], axis=0).astype(up.dtype)


def unit_backward(gate_sum, up_sum, back_sum, slot_prob):
    gate_sigmoid = jax.nn.sigmoid(gate_sum)
    gate_silu = gate_sum * gate_sigmoid
    prob_part = jnp.sum(gate_silu * up_sum * back_sum, axis=1)
    scaled_back = slot_prob[:, None] * back_sum
    gate_grad = (
        scaled_back * up_sum * gate_sigmoid * (1.0 + gate_sum * (1.0 - gate_sigmoid))
    ).astype(jnp.bfloat16)
    up_grad = (scaled_back * gate_silu).astype(jnp.bfloat16)
    return (gate_grad, up_grad, prob_part)


def local(
    logits,
    head_weight,
    token_ids,
    slab_order,
    token_weights,
    moe_input,
    routes,
    probs,
    w_gate,
    w_up,
    w_down,
):
    ctx_count = lax.axis_size("ctx")
    exp_count = lax.axis_size("exp")
    row_count, vocab_width = logits.shape
    seq_length = row_count * ctx_count
    all_logits = lax.all_gather(logits, "ctx", axis=0, tiled=True)

    token_count, route_count = routes.shape
    feature_width = moe_input.shape[1]
    capacity = min(token_count, 2 * token_count * route_count // exp_count)
    slot_count = exp_count * capacity
    tokens = jnp.arange(token_count, dtype=jnp.int32)
    experts = jnp.arange(exp_count, dtype=jnp.int32)
    named = routes.T[None] == experts[:, None, None]
    named_once = jnp.sum(named.astype(jnp.float32), axis=1)
    earlier = (tokens[:, None] < tokens[None, :]).astype(jnp.bfloat16)
    place = jnp.dot(named_once.astype(jnp.bfloat16), earlier, preferred_element_type=jnp.float32)
    place = jnp.where(named_once > 0, place, -1.0)
    held = place[:, None, :] == jnp.arange(capacity, dtype=jnp.float32)[None, :, None]
    slot_owner = held.astype(jnp.bfloat16).reshape(slot_count, token_count)

    scores = logits.astype(jnp.float32)
    local_max = jnp.max(scores, axis=1)
    local_sum = jnp.sum(jnp.exp(scores - local_max[:, None]), axis=1)
    expert_prob = jnp.sum(jnp.where(named, probs.astype(jnp.float32).T[None], 0.0), axis=1)
    send_prob = jnp.sum(jnp.where(held, expert_prob[:, None, :], 0.0), axis=2).astype(jnp.bfloat16)
    send_input = jnp.dot(slot_owner, moe_input, preferred_element_type=jnp.float32).astype(
        jnp.bfloat16
    )
    sum_high, sum_rest = split_high(local_sum)
    sum_mid, sum_low = split_high(sum_rest)
    stats = jnp.stack([local_max, sum_high, sum_mid, sum_low]).astype(jnp.bfloat16)
    extra = jnp.concatenate(
        [
            jnp.broadcast_to(stats[None], (exp_count, 4, row_count)),
            jnp.pad(
                send_prob.reshape(exp_count, 1, capacity),
                ((0, 0), (0, capacity - 5), (0, row_count - capacity)),
            ),
        ],
        axis=1,
    ).reshape(slot_count, row_count)
    got = exchange(jnp.concatenate([send_input, extra], axis=1), "exp")
    flat_inputs = got[:, :feature_width]
    extra = got[:, feature_width:].reshape(exp_count, capacity, row_count)
    flat_prob = extra[:, 4, :capacity].reshape(-1).astype(jnp.float32)
    stats = extra[:, :4].astype(jnp.float32)
    all_max = stats[:, 0]
    row_max = jnp.max(all_max, axis=0)
    row_total = jnp.sum(
        (stats[:, 1] + stats[:, 2] + stats[:, 3]) * jnp.exp(all_max - row_max), axis=0
    )
    own_ids = token_ids.astype(jnp.float32)
    later_id = lax.ppermute(
        own_ids[:1], "ctx", [((i + 1) % ctx_count, i) for i in range(ctx_count)]
    )
    own_next = jnp.concatenate([own_ids[1:], later_id])
    rows = jnp.concatenate([row_max, row_total, token_weights, own_next])
    rows = exchange(jnp.broadcast_to(rows[None], (ctx_count, 4 * row_count)), "ctx")
    rows = rows.reshape(ctx_count, 4, row_count).transpose(1, 0, 2).reshape(4, seq_length)
    rows, all_logits = lax.optimization_barrier((rows, all_logits))

    gate_w = w_gate[0]
    up_w = w_up[0]
    down_w = w_down[0]
    row_max, row_total, weights = rows[0], rows[1], rows[2]
    all_next = rows[3].astype(jnp.int32)

    one = 1 - jnp.minimum(lax.axis_index("ctx"), 0)
    head_weight = lax.optimization_barrier(head_weight * one.astype(jnp.bfloat16))

    slab_count = slab_order.shape[0]
    next_ids = all_next.reshape(slab_count, SLAB)
    slab_match = slab_order[:, None] == jnp.arange(slab_count, dtype=jnp.int32)[None, :]
    target = jnp.sum(jnp.where(slab_match[:, :, None], next_ids[None], 0), axis=1).reshape(-1)
    position = (slab_order[:, None] * SLAB + jnp.arange(SLAB, dtype=jnp.int32)).reshape(-1)
    has_target = position < seq_length - 1
    local_target = target - lax.axis_index("exp") * vocab_width
    weighting = jnp.where(has_target, weights, 0.0)
    columns = jnp.arange(vocab_width, dtype=jnp.int32)[None, :]
    per_row = jnp.stack([row_max, row_total, weighting, local_target.astype(jnp.float32)])

    def upstream_block(q, per_row):
        count = seq_length // NY
        top, total, weight, aim = lax.dynamic_slice_in_dim(per_row, q * count, count, axis=1)
        is_target = columns == aim.astype(jnp.int32)[:, None]
        logit_grads = (
            weight[:, None]
            * (
                jnp.exp(rows_at(all_logits, q, count).astype(jnp.float32) - top[:, None])
                / total[:, None]
                - is_target.astype(jnp.float32)
            )
        ).astype(jnp.bfloat16)
        partial = jnp.dot(logit_grads, head_weight, preferred_element_type=jnp.float32)
        return (partial * 4096.0).astype(jnp.float16)

    far = upstream_block((lax.axis_index("exp") // NZ + 2) % NY, per_row)
    far, flat_inputs = lax.optimization_barrier((far, flat_inputs))
    over_y = ring_sum_over_y(upstream_block, far, per_row)
    part_both = jnp.concatenate(
        [
            jnp.dot(flat_inputs, weight, preferred_element_type=jnp.float32).astype(jnp.float16)
            for weight in (gate_w, up_w)
        ],
        axis=1,
    )
    both_sum = ctx_scatter(part_both)
    upstream = exchange_sum(over_y, "exp", Z_GROUPS, NZ) * (1.0 / 4096.0)
    upstream_sent = upstream.astype(jnp.bfloat16)

    send_upstream = jnp.dot(slot_owner, upstream_sent, preferred_element_type=jnp.float32).astype(
        jnp.bfloat16
    )
    flat_upstream = exchange(send_upstream, "exp")
    flat_upstream, both_sum = lax.optimization_barrier((flat_upstream, both_sum))
    part_back = lax.dot_general(
        flat_upstream, down_w, CONTRACT_LAST, preferred_element_type=jnp.float32
    )
    back_sum = ctx_scatter(part_back)

    hidden = w_gate.shape[2]
    own_count = slot_count // ctx_count
    ctx_index = lax.axis_index("ctx")
    own_prob = rows_at(flat_prob, ctx_index % 2 * 4 + ctx_index // 2, own_count)
    gate_grad, up_grad, prob_grad = unit_backward(
        both_sum[:, :hidden], both_sum[:, hidden:], back_sum, own_prob
    )
    prob_high, prob_low = split_high(prob_grad)
    lane = jnp.arange(128, dtype=jnp.int32)[None, :]
    prob_block = jnp.where(
        lane == 0, prob_high[:, None], jnp.where(lane == 1, prob_low[:, None], 0)
    ).astype(jnp.bfloat16)
    def route_gradients(grads):
        input_grad = lax.dot_general(
            grads[:, :hidden], gate_w, CONTRACT_LAST, preferred_element_type=jnp.float32
        ) + lax.dot_general(
            grads[:, hidden : 2 * hidden], up_w, CONTRACT_LAST, preferred_element_type=jnp.float32
        )
        return jnp.concatenate([input_grad.astype(jnp.bfloat16), grads[:, 2 * hidden :]], axis=1)

    grads = chips_gather(jnp.concatenate([gate_grad, up_grad, prob_block], axis=1))
    other_grads = ctx_swap(grads)
    mine, others = route_gradients(grads), route_gradients(other_grads)
    core = lax.axis_index("ctx") % 2
    send_back = jnp.concatenate(
        [jnp.where(core == 0, mine, others), jnp.where(core == 0, others, mine)], axis=0
    )
    back = exchange(send_back, "exp")
    d_x = upstream + lax.dot_general(
        slot_owner,
        back[:, :feature_width],
        (((0,), (0,)), ((), ())),
        preferred_element_type=jnp.float32,
    )
    back_prob = back[:, feature_width : feature_width + 2].astype(jnp.float32)
    back_prob = (back_prob[:, 0] + back_prob[:, 1]).reshape(exp_count, capacity)
    token_prob = jnp.sum(jnp.where(held, back_prob[:, :, None], 0.0), axis=1)
    d_prob = jnp.sum(jnp.where(named, token_prob[:, None, :], 0.0), axis=0).T
    return (d_x, d_prob)


def solution(mesh):
    placed = (
        P("ctx", "exp"),
        P("exp", "ctx"),
        P("ctx"),
        P(),
        P("ctx"),
        P("exp", "ctx"),
        P("exp", None),
        P("exp", None),
        P("exp", "ctx", None),
        P("exp", "ctx", None),
        P("exp", None, "ctx"),
    )
    return jax.shard_map(
        local,
        mesh=mesh,
        in_specs=placed,
        out_specs=(P("exp", "ctx"), P("exp", None)),
        check_vma=False,
    )
```
